128 devices in a mesh: group: 8 (over x, y_hi), shard: 16 (over z, y_lo, core).
Axes of the slice: x: 4, y: 4 (y_hi: 2, y_lo: 2; y = y_hi * 2 + y_lo), z: 4, core: 2. Of those that a mesh axis runs over, the one named last changes fastest.
Arguments:
- images: bfloat16 [128, 28, 28, 512], P(('group', 'shard')), may hold values from -6 to 6
- cotangent: bfloat16 [128, 28, 28, 512], P(('group', 'shard')), may hold values from -6 to 6
- dw_kernel: bfloat16 [49, 512], P(None, 'shard'), may hold values from -0.875 to 0.875
- norm_gain: float32 [512], replicated, may hold values from 0.1 to 1.9
- w_up: bfloat16 [512, 2048], P('shard'), may hold values from -0.25 to 0.25
- w_down: bfloat16 [2048, 512], P('shard'), may hold values from -0.125 to 0.125
- owner_table: int32 [8], replicated, may hold values from 0 to 7, each once
Outputs:
- mixed: bfloat16 [128, 28, 28, 512], P(('group', 'shard'))
- back_images: bfloat16 [128, 28, 28, 512], P(('group', 'shard'))
- statistics: float32 [8, 2, 512, 512], P('group')
The draws below stay inside these ranges and needn't reach their ends.
Inputs may be any that keep to these rules, and one draw needn't show every extreme that they name: `owner_table`: each of 0 to 7 stands once.
All inputs are finite; a program needn't handle non-finite values.
Results may differ from the reference program's by a relative error of at most 0.014.
Values may be sent and summed in bfloat16 or wider, within the bound.
A program may use at most 128 MiB of HBM per device.

```python
import jax
import jax.numpy as jnp
from jax import lax

C = 512
FF = 2048
BLK = 512
HH = 28
WW = 28
IMG_DEV = 1
IMAGES = 128
NBLK = 8
N_GROUP = 8
N_SHARD = 16


def levels(rng, extent, shards, least, largest):
    loudness, own = 1.0, jax.random.fold_in(rng, 6)
    for dim, blocks in shards:
        steps = jnp.exp(jax.random.uniform(jax.random.fold_in(own, dim), (blocks,), jnp.float32, least / len(shards), largest / len(shards)))
        loudness = loudness * jnp.repeat(steps, extent[dim] // blocks).reshape([-1 if axis == dim else 1 for axis in range(len(extent))])
    return loudness


def normal_values(rng, shape, deviation, limit, cuts=(), held_as=jnp.bfloat16):
    level = levels(rng, shape, cuts, -0.22, 0.18) if cuts else 1.0
    entries = jax.random.normal(rng, shape, jnp.float32) * deviation * level
    return jnp.minimum(jnp.maximum(entries, -limit), limit).astype(held_as)


def setup_inputs(seed: int = 0) -> dict:
    arg_keys = jax.random.split(jax.random.key(seed), 8)
    images = normal_values(arg_keys[0], (IMAGES, HH, WW, C), 1.0, 6.0, ((0, 128),))
    cotangent = normal_values(arg_keys[1], (IMAGES, HH, WW, C), 1.0, 6.0, ((0, 128),))
    dw_kernel = normal_values(arg_keys[2], (49, C), 49 ** -0.5, 0.875, ((1, 16),))
    norm_gain = jnp.clip(1.0 + 0.18 * jax.random.normal(arg_keys[3], (C,), jnp.float32), 0.1, 1.9)
    w_up = normal_values(arg_keys[4], (C, FF), C ** -0.5, 0.25, ((0, 16),))
    w_down = normal_values(arg_keys[5], (FF, C), FF ** -0.5, 0.125, ((0, 16),))
    owner_table = jax.random.permutation(arg_keys[6], NBLK).astype(jnp.int32)
    return {"images": images, "cotangent": cotangent, "dw_kernel": dw_kernel, "norm_gain": norm_gain, "w_up": w_up, "w_down": w_down, "owner_table": owner_table}


def normed_map(xfloat, kernel, gain):
    width = xfloat.shape[-1]
    taps = kernel.astype(jnp.float32).reshape(7, 7, 1, width)
    conv = lax.conv_general_dilated(xfloat, taps, (1, 1), 'SAME', dimension_numbers=('NHWC', 'HWIO', 'NHWC'), feature_group_count=width, precision=lax.Precision.HIGHEST)
    mean = lax.optimization_barrier(jnp.mean(conv, axis=-1, keepdims=True))
    var = lax.optimization_barrier(jnp.mean((conv - mean) ** 2, axis=-1, keepdims=True))
    return (conv - mean) / jnp.sqrt(var + 1e-06) * gain

def normal_cdf(v):
    return 0.5 * (1.0 + lax.erf(v * 0.7071067811865476))

def normal_pdf(v):
    return 0.3989422804014327 * jnp.exp(-0.5 * v * v)

def tiles_of(matrix, size):
    rows, cols = matrix.shape
    return matrix.reshape(rows // size, size, cols // size, size).transpose(0, 2, 1, 3).reshape(-1, size, size)

def group_pass(pair, dw_kernel, norm_gain, w_up, w_down):
    images, cotangent = pair
    width = images.shape[-1]
    xfloat = images.astype(jnp.float32)
    normed, pullback = jax.vjp(lambda v: normed_map(v, dw_kernel, norm_gain), xfloat)
    u = normed.astype(jnp.bfloat16).reshape(-1, width)
    pre = jnp.dot(u, w_up, preferred_element_type=jnp.float32)
    act = (pre * normal_cdf(pre)).astype(jnp.bfloat16)
    branch = jnp.dot(act, w_down, preferred_element_type=jnp.float32)
    mixed = (xfloat + branch.reshape(images.shape)).astype(jnp.bfloat16)
    back_rows = cotangent.reshape(-1, width)
    back_act = jnp.dot(back_rows, w_down.T, preferred_element_type=jnp.float32)
    back_pre = (back_act * (normal_cdf(pre) + pre * normal_pdf(pre))).astype(jnp.bfloat16)
    back_u = jnp.dot(back_pre, w_up.T, preferred_element_type=jnp.float32)
    back_x = pullback(back_u.reshape(images.shape))[0]
    back_images = (cotangent.astype(jnp.float32) + back_x).astype(jnp.bfloat16)
    scale = 1.0 / jnp.sqrt(jnp.float32(u.shape[0]))
    grad_up = jnp.dot(u.T, back_pre, preferred_element_type=jnp.float32) * scale
    grad_down = jnp.dot(act.T, back_rows, preferred_element_type=jnp.float32) * scale
    blocks = jnp.concatenate([tiles_of(grad_up, BLK), tiles_of(grad_down, BLK)], axis=0)
    left = jnp.einsum('kij,klj->kil', blocks, blocks, precision=lax.Precision.HIGHEST) / BLK
    right = jnp.einsum('kji,kjl->kil', blocks, blocks, precision=lax.Precision.HIGHEST) / BLK
    return (mixed, back_images, jnp.stack([left, right], axis=1))

def reference(images, cotangent, dw_kernel, norm_gain, w_up, w_down, owner_table):
    per_group = IMG_DEV * N_SHARD
    shaped = (N_GROUP, per_group, HH, WW, C)
    mixed, back_images, stats = lax.map(lambda pair: group_pass(pair, dw_kernel, norm_gain, w_up, w_down), (images.reshape(shaped), cotangent.reshape(shaped)))
    total = lax.optimization_barrier(jnp.sum(stats, axis=0))
    statistics = total[owner_table.astype(jnp.int32)]
    return (mixed.reshape(images.shape), back_images.reshape(images.shape), statistics)
```

```python
import functools

import jax
import jax.numpy as jnp
from jax import lax
from jax.experimental import pallas as pl
from jax.experimental.pallas import tpu as pltpu
from jax.sharding import PartitionSpec as P

BLK = 512


def normed_map(xfloat, kernel, gain):
    width = xfloat.shape[-1]
    taps = kernel.astype(jnp.float32).reshape(7, 7, 1, width)
    conv = lax.conv_general_dilated(
        xfloat,
        taps,
        (1, 1),
        "SAME",
        dimension_numbers=("NHWC", "HWIO", "NHWC"),
        feature_group_count=width,
        precision=lax.Precision.HIGHEST,
    )
    mean = jnp.mean(conv, axis=-1, keepdims=True)
    var = jnp.mean((conv - mean) ** 2, axis=-1, keepdims=True)
    return (conv - mean) / jnp.sqrt(var + 1e-06) * gain


def normal_cdf(v):
    return 0.5 * (1.0 + lax.erf(v * 0.7071067811865476))


def normal_pdf(v):
    return 0.3989422804014327 * jnp.exp(-0.5 * v * v)


def tiles_of(matrix, size):
    rows, cols = matrix.shape
    return (
        matrix.reshape(rows // size, size, cols // size, size)
        .transpose(0, 2, 1, 3)
        .reshape(-1, size, size)
    )


MESH = pl.DeviceIdType.MESH


def stats_kernel(n, tile, p_ref, out_ref, a0, q, a1, gfull, m, c1, ag, a0s, a0r, a1s, a1r, gs, gr, cs, cr, ds, dr, es, er, fs, fr):
    g, s = lax.axis_index("group"), lax.axis_index("shard")
    core, pair = lax.rem(s, 2), lax.div(s, 2)
    sib = s + 1 - 2 * core
    half, chunk = tile // 2, tile // n
    f32, bf16 = jnp.float32, jnp.bfloat16

    def dma(src, dst, ssem, rsem, group, shard):
        return pltpu.make_async_remote_copy(
            src_ref=src, dst_ref=dst, send_sem=ssem, recv_sem=rsem, device_id=(group, shard), device_id_type=MESH
        )

    target = (pair, 2 * lax.rem(g + 1, n) + core)
    source = (lax.rem(pair + n - 1, n), 2 * g + core)
    barrier = pltpu.get_barrier_semaphore()

    def greet(group, shard):
        pl.semaphore_signal(barrier, inc=1, device_id=(group, shard), device_id_type=MESH)

    greet(g, sib)
    for i in range(1, n):
        greet(g, 2 * lax.rem(pair + i, n) + core)
        greet(lax.rem(g + i, n), s)
    greet(*target)
    greet(*source)
    pl.semaphore_wait(barrier, 2 * n + 1)

    own = pl.ds(pl.multiple_of(core * half, half), half)
    other = pl.ds(pl.multiple_of((1 - core) * half, half), half)

    def slot(i):
        return lax.rem(pair + 1 + i, n)

    def a0_copy(i):
        return dma(p_ref.at[slot(i), other], a0.at[i], a0s.at[i], a0r.at[i], g, sib)

    def a1_copy(i):
        return dma(q.at[i], a1.at[i], a1s.at[i], a1r.at[i], g, 2 * slot(i) + core)

    @pl.loop(0, n)
    def _(i):
        a0_copy(i).start()

    @pl.loop(0, n - 1)
    def _(i):
        a0_copy(i).wait_recv()
        q[i] = (p_ref[slot(i), own].astype(f32) + a0[i].astype(f32)).astype(bf16)
        a1_copy(i).start()

    a0_copy(n - 1).wait_recv()
    acc = p_ref[pair, own].astype(f32) + a0[n - 1].astype(f32)
    for i in range(n - 1):
        a1_copy(i).wait_recv()
        acc = acc + a1[i].astype(f32)
    gfull[own] = acc.astype(bf16)
    g_copy = dma(gfull.at[own], gfull.at[own], gs, gr, g, sib)
    g_copy.start()
    g_copy.wait_recv()
    whole = gfull[...]
    side = jnp.where(core == 0, whole, whole.T)
    stat = lax.dot_general(side, side, (((1,), (1,)), ((), ())), preferred_element_type=f32)
    m[...] = (stat * (1.0 / tile)).astype(bf16).reshape(n, chunk, tile)

    def c_copy(i):
        j = lax.rem(g + i, n)
        return dma(m.at[j], c1.at[i], cs.at[i], cr.at[i], j, s)

    for i in range(1, n):
        c_copy(i).start()
    acc = m[g].astype(f32)
    for i in range(1, n):
        c_copy(i).wait_recv()
        acc = acc + c1[i].astype(f32)
    c1[0] = acc.astype(bf16)
    d_copy = dma(c1.at[0], ag.at[target[1]], ds, dr, *target)
    d_copy.start()
    dma(c1.at[0], ag.at[s], ds, dr, *target).wait_recv()

    def e_copy(i):
        return dma(ag.at[s], ag.at[s], es.at[i], er.at[i], g, 2 * lax.rem(pair + i, n) + core)

    def f_copy(i):
        j = 2 * lax.rem(pair + n - i, n) + core
        return dma(ag.at[j], ag.at[j], fs.at[i], fr.at[i], g, sib)

    for i in range(1, n):
        e_copy(i).start()
    f_copy(0).start()
    for i in range(1, n):
        e_copy(i).wait_recv()
        f_copy(i).start()
    for i in range(n):
        f_copy(i).wait_recv()
    for k in range(2 * n):
        out_ref[k % 2, pl.ds((k // 2 + n - 1) % n * chunk, chunk)] = ag[k].astype(f32)

    for i in range(n):
        a0_copy(i).wait_send()
        f_copy(i).wait_send()
    for i in range(n - 1):
        a1_copy(i).wait_send()
        c_copy(i + 1).wait_send()
        e_copy(i + 1).wait_send()
    g_copy.wait_send()
    d_copy.wait_send()


def group_statistics(parts, n):
    tile = parts.shape[-1]
    half, chunk = tile // 2, tile // n
    bf16 = jnp.bfloat16
    dma_sem = pltpu.SemaphoreType.DMA
    return pl.pallas_call(
        functools.partial(stats_kernel, n, tile),
        out_shape=jax.ShapeDtypeStruct((2, tile, tile), jnp.float32),
        in_specs=[pl.BlockSpec(memory_space=pltpu.VMEM)],
        out_specs=pl.BlockSpec(memory_space=pltpu.VMEM),
        scratch_shapes=[
            pltpu.VMEM((n, half, tile), bf16),
            pltpu.VMEM((n - 1, half, tile), bf16),
            pltpu.VMEM((n - 1, half, tile), bf16),
            pltpu.VMEM((tile, tile), bf16),
            pltpu.VMEM((n, chunk, tile), bf16),
            pltpu.VMEM((n, chunk, tile), bf16),
            pltpu.VMEM((2 * n, chunk, tile), bf16),
            dma_sem((n,)), dma_sem((n,)),
            dma_sem((n - 1,)), dma_sem((n - 1,)),
            dma_sem, dma_sem,
            dma_sem((n,)), dma_sem((n,)),
            dma_sem, dma_sem,
            dma_sem((n,)), dma_sem((n,)),
            dma_sem((n,)), dma_sem((n,)),
        ],
        compiler_params=pltpu.CompilerParams(collective_id=0, has_side_effects=True, vmem_limit_bytes=40 * 2**20),
    )(parts)


def local(images, cotangent, dw_kernel, norm_gain, w_up, w_down, owner_table):
    kernel, up_full, down_full = (
        lax.all_gather(dw_kernel, "shard", axis=1, tiled=True),
        lax.all_gather(w_up, "shard", axis=0, tiled=True),
        lax.all_gather(w_down, "shard", axis=0, tiled=True),
    )
    width = images.shape[-1]
    xfloat = images.astype(jnp.float32)
    normed, pullback = jax.vjp(lambda v: normed_map(v, kernel, norm_gain), xfloat)
    u = normed.astype(jnp.bfloat16).reshape(-1, width)
    pre = jnp.dot(u, up_full, preferred_element_type=jnp.float32)
    act = (pre * normal_cdf(pre)).astype(jnp.bfloat16)
    branch = jnp.dot(act, down_full, preferred_element_type=jnp.float32)
    mixed = (xfloat + branch.reshape(images.shape)).astype(jnp.bfloat16)
    back_rows = cotangent.reshape(-1, width)
    back_act = lax.dot_general(
        back_rows, down_full, (((1,), (1,)), ((), ())), preferred_element_type=jnp.float32
    )
    back_pre = (back_act * (normal_cdf(pre) + pre * normal_pdf(pre))).astype(jnp.bfloat16)
    back_u = lax.dot_general(
        back_pre, up_full, (((1,), (1,)), ((), ())), preferred_element_type=jnp.float32
    )
    back_x = pullback(back_u.reshape(images.shape))[0]
    back_images = (cotangent.astype(jnp.float32) + back_x).astype(jnp.bfloat16)
    group_rows = u.shape[0] * lax.axis_size("shard")
    scale = 1.0 / jnp.sqrt(jnp.float32(group_rows))
    part_up = (
        lax.dot_general(u, back_pre, (((0,), (0,)), ((), ())), preferred_element_type=jnp.float32)
        * scale
    )
    part_down = (
        lax.dot_general(
            act, back_rows, (((0,), (0,)), ((), ())), preferred_element_type=jnp.float32
        )
        * scale
    )
    blocks = jnp.concatenate(
        [tiles_of(part_up.astype(jnp.bfloat16), BLK), tiles_of(part_down.astype(jnp.bfloat16), BLK)], axis=0
    )
    ordered = jnp.take(blocks, owner_table, axis=0)
    statistics = group_statistics(ordered, lax.axis_size("group"))[None]
    return (mixed, back_images, statistics)


def solution(mesh):
    return jax.shard_map(
        local,
        mesh=mesh,
        in_specs=(
            P(("group", "shard"), None, None, None),
            P(("group", "shard"), None, None, None),
            P(None, "shard"),
            P(),
            P("shard", None),
            P("shard", None),
            P(),
        ),
        out_specs=(
            P(("group", "shard"), None, None, None),
            P(("group", "shard"), None, None, None),
            P("group", None, None, None),
        ),
        check_vma=False,
    )
```

```python
import functools

import jax
import jax.numpy as jnp
from jax import lax
from jax.experimental import pallas as pl
from jax.experimental.pallas import tpu as pltpu
from jax.sharding import PartitionSpec as P

BLK = 512
F32, BF16 = jnp.float32, jnp.bfloat16
ROWS, COLS, HALO = 28, 28, 3
PIX = ROWS * COLS
HROWS = ROWS // 2
XROWS, XCOLS = HROWS + 2 * HALO, COLS + 2 * HALO
NT = (((1,), (1,)), ((), ()))
TN = (((0,), (0,)), ((), ()))


def at8(start, size):
    return pl.ds(pl.multiple_of(start, 8), size)


def put_row(x2, half, row, line):
    for blk in range(4):
        start = (row * XCOLS + HALO) * 8 + half * 4 + blk
        x2[pl.ds(start, COLS, stride=8), :] = line[:, 128 * blk : 128 * blk + 128]


def fill_images(x2, img):
    x2[...] = jnp.zeros_like(x2)

    @pl.loop(0, HROWS + HALO)
    def _(i):
        put_row(x2, 0, i + HALO, img[i].astype(F32))
        put_row(x2, 1, i, img[i + HROWS - HALO].astype(F32))


def conv_row(x2, w2, c2, h, flip):
    for w0 in range(0, COLS, 14):
        acc = jnp.zeros((14, 8, 128), F32)
        for a in range(7):
            row = x2[at8(((h + a) * XCOLS + w0) * 8, 160), :].reshape(20, 8, 128)
            for b in range(7):
                tap = 48 - 7 * a - b if flip else 7 * a + b
                acc = acc + row[b : b + 14] * w2[8 * tap : 8 * tap + 8, :][None]
        c2[at8((h * COLS + w0) * 8, 112), :] = acc.reshape(112, 128)


def norm_rows(c2, xhat, rstd):
    @pl.loop(0, 7)
    def _(k):
        for half in range(2):
            parts = [c2[pl.ds(k * 448 + half * 4 + blk, 56, stride=8), :] for blk in range(4)]
            mean = jnp.sum(parts[0] + parts[1] + parts[2] + parts[3], axis=1, keepdims=True) * (1.0 / 512)
            parts = [v - mean for v in parts]
            sq = [v * v for v in parts]
            var = jnp.sum(sq[0] + sq[1] + sq[2] + sq[3], axis=1, keepdims=True) * (1.0 / 512)
            inv = 1.0 / jnp.sqrt(var + 1e-06)
            rows = at8(half * 392 + k * 56, 56)
            for blk in range(4):
                xhat[rows, 128 * blk : 128 * blk + 128] = parts[blk] * inv
            rstd[rows, :] = jnp.broadcast_to(inv, (56, 128))


def scale_rows(xhat, gain, lhs):
    @pl.loop(0, 7)
    def _(k):
        rows = pl.ds(pl.multiple_of(k * 112, 16), 112)
        lhs[0, rows, :] = (xhat[rows, :] * gain[...]).astype(BF16)


def flat_rows(cot, rhs):
    @pl.loop(0, 7)
    def _(k):
        lines = [cot[4 * k + r].astype(F32) for r in range(4)]
        rhs[4, pl.ds(pl.multiple_of(k * 112, 16), 112), :] = jnp.concatenate(lines, axis=0).astype(BF16)


def gelu_pair(v):
    cdf = 0.5 * (1.0 + lax.erf(v * 0.7071067811865476))
    pdf = 0.3989422804014327 * jnp.exp(-0.5 * v * v)
    return v * cdf, cdf + v * pdf


def up_step(lhs, up, slope, j):
    cols = pl.ds(pl.multiple_of(j * 256, 256), 256)
    part = pl.ds(pl.multiple_of(lax.rem(j, 2) * 256, 256), 256)
    pre = jnp.dot(lhs[0], up[:, cols], preferred_element_type=F32)
    act, der = gelu_pair(pre)
    lhs[1 + lax.div(j, 2), :, part] = act.astype(BF16)
    slope[j] = der


def back_step(rhs, down, slope, j):
    rows = pl.ds(pl.multiple_of(j * 256, 256), 256)
    part = pl.ds(pl.multiple_of(lax.rem(j, 2) * 256, 256), 256)
    back = lax.dot_general(rhs[4], down[rows, :], NT, preferred_element_type=F32)
    rhs[lax.div(j, 2), :, part] = (back * slope[j]).astype(BF16)


def grad_tile(lhs, rhs, k, scale):
    left = jnp.maximum(k - 3, 0)
    right = jnp.minimum(k, 4)
    return lax.dot_general(lhs[left], rhs[right], TN, preferred_element_type=F32) * scale


def branch_cols(lhs, down, out, j):
    cols = pl.ds(pl.multiple_of(j * 256, 256), 256)
    acc = jnp.dot(lhs[1], down[0:512, cols], preferred_element_type=F32)
    for k in range(1, 4):
        acc = acc + jnp.dot(lhs[1 + k], down[512 * k : 512 * k + 512, cols], preferred_element_type=F32)
    out[:, cols] = acc


def back_u_cols(rhs, up, out, j):
    rows = pl.ds(pl.multiple_of(j * 256, 256), 256)
    acc = lax.dot_general(rhs[0], up[rows, 0:512], NT, preferred_element_type=F32)
    for k in range(1, 4):
        acc = acc + lax.dot_general(rhs[k], up[rows, 512 * k : 512 * k + 512], NT, preferred_element_type=F32)
    out[:, rows] = acc


def mix_rows(img, branch, mixed):
    @pl.loop(0, 14)
    def _(k):
        lines = branch[at8(k * 56, 56), :]
        for r in range(2):
            mixed[2 * k + r] = (img[2 * k + r].astype(F32) + lines[28 * r : 28 * r + 28]).astype(BF16)


def norm_back_rows(back, xhat, rstd, gain):
    @pl.loop(0, 14)
    def _(k):
        rows = at8(k * 56, 56)
        grad = back[rows, :] * gain[...]
        unit = xhat[rows, :]
        first = jnp.sum(grad, axis=1, keepdims=True) * (1.0 / 512)
        second = jnp.sum(grad * unit, axis=1, keepdims=True) * (1.0 / 512)
        back[rows, :] = rstd[rows, 0:1] * (grad - first - unit * second)


def fill_back(x2, back):
    @pl.loop(0, 8)
    def _(i):
        lines = back[at8(i * 56, 56), :]
        for r in range(2):
            put_row(x2, 0, 2 * i + r + HALO, lines[28 * r : 28 * r + 28])
        lines = back[at8((i + 6) * 56, 56), :]
        for r in range(2):
            put_row(x2, 1, 2 * i + r + 1, lines[28 * r : 28 * r + 28])

    put_row(x2, 0, 16 + HALO, back[448:476, :])
    put_row(x2, 1, 0, back[308:336, :])


def conv_back_rows(x2, w2, c2, cot, out):
    @pl.loop(0, HROWS)
    def _(h):
        conv_row(x2, w2, c2, h, True)
        for half in range(2):
            line = [c2[pl.ds(h * COLS * 8 + half * 4 + blk, COLS, stride=8), :] for blk in range(4)]
            back = jnp.concatenate(line, axis=1)
            out[half * HROWS + h] = (cot[half * HROWS + h].astype(F32) + back).astype(BF16)


MESH = pl.DeviceIdType.MESH


def block_kernel(
    n, img, cot, dw, gain, up_in, down_in, owner,
    mixed, out, stat_out,
    x2, w2, c2, xhat, rstd, lhs, rhs, up, down, slope, wide, dwb, p, a0, q, a1, gfull, m, c1, ag,
    dws, dwr, ups, upr, downs, downr, a0s, a0r, a1s, a1r, gs, gr, cs, cr, ds, dr, es, er,
):
    g, s = lax.axis_index("group"), lax.axis_index("shard")
    core, pair = lax.rem(s, 2), lax.div(s, 2)
    sib = s + 1 - 2 * core
    tile = BLK
    half, chunk = tile // 2, tile // n

    def dma(src, dst, ssem, rsem, group, shard):
        return pltpu.make_async_remote_copy(
            src_ref=src, dst_ref=dst, send_sem=ssem, recv_sem=rsem, device_id=(group, shard), device_id_type=MESH
        )

    def peer(i):
        return 2 * lax.rem(pair + i, n) + core

    def gather(mine, place, send, recv):
        def out_copy(i):
            return dma(mine, place(s), send.at[0, i], recv.at[0, i], g, peer(i))

        def on_copy(i):
            j = peer(n - i)
            return dma(mine if i == 0 else place(j), place(s if i == 0 else j), send.at[1, i], recv.at[1, i], g, sib)

        def start():
            on_copy(0).start()
            for i in range(1, n):
                out_copy(i).start()

        def forward():
            for i in range(1, n):
                out_copy(i).wait_recv()
                on_copy(i).start()

        def arrived():
            for i in range(n):
                on_copy(i).wait_recv()

        def finish():
            on_copy(0).wait_send()
            for i in range(1, n):
                out_copy(i).wait_send()
                on_copy(i).wait_send()

        return start, forward, arrived, finish

    target = (pair, 2 * lax.rem(g + 1, n) + core)
    source = (lax.rem(pair + n - 1, n), 2 * g + core)
    barrier = pltpu.get_barrier_semaphore()

    def greet(group, shard):
        pl.semaphore_signal(barrier, inc=1, device_id=(group, shard), device_id_type=MESH)

    for i in range(1, 2 * n):
        greet(g, lax.rem(s + i, 2 * n))
    for i in range(1, n):
        greet(lax.rem(g + i, n), s)
    greet(*target)
    greet(*source)

    taps = dw[...].astype(F32)
    taps = jnp.concatenate([taps, taps, taps, taps], axis=1)
    lane = lax.broadcasted_iota(jnp.int32, taps.shape, 1)
    low = 32 * lax.rem(s, 4)
    taps = jnp.where((lane >= low) & (lane < low + 32), taps, 0.0)
    dwb[s] = jnp.zeros((64, 128), BF16)
    dwb[s, 0:49, :] = taps.astype(BF16)
    up[pl.ds(pl.multiple_of(s * 32, 32), 32), :] = up_in[...]
    down[pl.ds(pl.multiple_of(s * 128, 128), 128), :] = down_in[...]
    fill_images(x2, img)

    up_start, up_forward, up_arrived, up_finish = gather(
        up_in, lambda j: up.at[pl.ds(pl.multiple_of(j * 32, 32), 32)], ups, upr
    )
    down_start, down_forward, down_arrived, down_finish = gather(
        down_in, lambda j: down.at[pl.ds(pl.multiple_of(j * 128, 128), 128)], downs, downr
    )
    ag_start, ag_forward, ag_arrived, ag_finish = gather(ag.at[s], lambda j: ag.at[j], es, er)

    def dw_copy(i):
        return dma(dwb.at[s], dwb.at[s], dws.at[i], dwr.at[i], g, lax.rem(s + i, 2 * n))

    pl.semaphore_wait(barrier, 3 * n)
    for i in range(1, 2 * n):
        dw_copy(i).start()
    up_start()
    flat_rows(cot, rhs)
    for i in range(1, 2 * n):
        dw_copy(i).wait_recv()
    for blk in range(4):
        lines = [dwb[4 * blk + t].astype(F32) for t in range(4)]
        line = lines[0] + lines[1] + lines[2] + lines[3]
        w2[pl.ds(blk, 64, stride=8), :] = line
        w2[pl.ds(blk + 4, 64, stride=8), :] = line

    @pl.loop(0, 7)
    def _(h):
        conv_row(x2, w2, c2, h, False)

    down_start()

    @pl.loop(7, HROWS)
    def _(h):
        conv_row(x2, w2, c2, h, False)

    norm_rows(c2, xhat, rstd)
    scale_rows(xhat, gain, lhs)
    up_forward()
    up_arrived()

    @pl.loop(0, 8)
    def _(j):
        up_step(lhs, up, slope, j)

    down_forward()
    down_arrived()

    @pl.loop(0, 8)
    def _(j):
        back_step(rhs, down, slope, j)

    own = pl.ds(pl.multiple_of(core * half, half), half)
    other = pl.ds(pl.multiple_of((1 - core) * half, half), half)
    scale = (2 * n * PIX) ** -0.5

    def slot(i):
        return lax.rem(pair + 1 + i, n)

    def a0_copy(i):
        return dma(p.at[i, other], a0.at[i], a0s.at[i], a0r.at[i], g, sib)

    def a1_copy(i):
        return dma(q.at[i], a1.at[i], a1s.at[i], a1r.at[i], g, 2 * slot(i) + core)

    def pass_on(i):
        a0_copy(i).wait_recv()
        q[i] = (p[i, own].astype(F32) + a0[i].astype(F32)).astype(BF16)
        a1_copy(i).start()

    @pl.loop(0, n)
    def _(i):
        p[i] = grad_tile(lhs, rhs, owner[slot(i)], scale).astype(BF16)
        a0_copy(i).start()

        @pl.when(i > 0)
        def _():
            pass_on(i - 1)

    @pl.loop(0, 2)
    def _(j):
        branch_cols(lhs, down, wide, j)

    mix_rows(img, wide, mixed)

    @pl.loop(0, 2)
    def _(j):
        back_u_cols(rhs, up, wide, j)

    norm_back_rows(wide, xhat, rstd, gain)
    fill_back(x2, wide)
    conv_back_rows(x2, w2, c2, cot, out)

    a0_copy(n - 1).wait_recv()
    acc = p[n - 1, own].astype(F32) + a0[n - 1].astype(F32)
    for i in range(n - 1):
        a1_copy(i).wait_recv()
        acc = acc + a1[i].astype(F32)
    gfull[own] = acc.astype(BF16)
    g_copy = dma(gfull.at[own], gfull.at[own], gs, gr, g, sib)
    g_copy.start()
    g_copy.wait_recv()
    whole = gfull[...]
    side = jnp.where(core == 0, whole, whole.T)
    stat = lax.dot_general(side, side, NT, preferred_element_type=F32)
    m[...] = (stat * (1.0 / tile)).astype(BF16).reshape(n, chunk, tile)

    def c_copy(i):
        j = lax.rem(g + i, n)
        return dma(m.at[j], c1.at[i], cs.at[i], cr.at[i], j, s)

    for i in range(1, n):
        c_copy(i).start()
    acc = m[g].astype(F32)
    for i in range(1, n):
        c_copy(i).wait_recv()
        acc = acc + c1[i].astype(F32)
    c1[0] = acc.astype(BF16)
    d_copy = dma(c1.at[0], ag.at[target[1]], ds, dr, *target)
    d_copy.start()
    d_copy.wait_recv()
    ag_start()
    ag_forward()
    ag_arrived()
    for k in range(2 * n):
        stat_out[k % 2, pl.ds((k // 2 + n - 1) % n * chunk, chunk)] = ag[k].astype(F32)

    up_finish()
    down_finish()
    ag_finish()
    for i in range(1, 2 * n):
        dw_copy(i).wait_send()
    for i in range(n):
        a0_copy(i).wait_send()
    for i in range(n - 1):
        a1_copy(i).wait_send()
        c_copy(i + 1).wait_send()
    g_copy.wait_send()
    d_copy.wait_send()


def local(images, cotangent, dw_kernel, norm_gain, w_up, w_down, owner_table):
    n = lax.axis_size("group")
    half, chunk = BLK // 2, BLK // n
    sem = pltpu.SemaphoreType.DMA
    vmem = pltpu.VMEM
    width = images.shape[-1]
    mixed, back, stat = pl.pallas_call(
        functools.partial(block_kernel, n),
        out_shape=(
            jax.ShapeDtypeStruct((ROWS, COLS, width), BF16),
            jax.ShapeDtypeStruct((ROWS, COLS, width), BF16),
            jax.ShapeDtypeStruct((2, BLK, BLK), F32),
        ),
        in_specs=[pl.BlockSpec(memory_space=vmem)] * 6 + [pl.BlockSpec(memory_space=pltpu.SMEM)],
        out_specs=[pl.BlockSpec(memory_space=vmem)] * 3,
        scratch_shapes=[
            vmem((XROWS * XCOLS * 8, 128), F32),
            vmem((512, 128), F32),
            vmem((HROWS * COLS * 8, 128), F32),
            vmem((PIX, width), F32),
            vmem((PIX, 128), F32),
            vmem((5, PIX, width), BF16),
            vmem((5, PIX, width), BF16),
            vmem((512, 2048), BF16),
            vmem((2048, 512), BF16),
            vmem((8, PIX, 256), F32),
            vmem((PIX, width), F32),
            vmem((2 * n, 64, 128), BF16),
            vmem((n, BLK, BLK), BF16),
            vmem((n, half, BLK), BF16),
            vmem((n - 1, half, BLK), BF16),
            vmem((n - 1, half, BLK), BF16),
            vmem((BLK, BLK), BF16),
            vmem((n, chunk, BLK), BF16),
            vmem((n, chunk, BLK), BF16),
            vmem((2 * n, chunk, BLK), BF16),
            sem((2 * n,)), sem((2 * n,)),
            sem((2, n)), sem((2, n)),
            sem((2, n)), sem((2, n)),
            sem((n,)), sem((n,)),
            sem((n - 1,)), sem((n - 1,)),
            sem, sem,
            sem((n,)), sem((n,)),
            sem, sem,
            sem((2, n)), sem((2, n)),
        ],
        compiler_params=pltpu.CompilerParams(collective_id=0, has_side_effects=True, vmem_limit_bytes=60 * 2**20),
    )(images[0], cotangent[0], dw_kernel, norm_gain.reshape(1, width), w_up, w_down, owner_table)
    return (mixed[None], back[None], stat[None])


def solution(mesh):
    return jax.shard_map(
        local,
        mesh=mesh,
        in_specs=(
            P(("group", "shard"), None, None, None),
            P(("group", "shard"), None, None, None),
            P(None, "shard"),
            P(),
            P("shard", None),
            P("shard", None),
            P(),
        ),
        out_specs=(
            P(("group", "shard"), None, None, None),
            P(("group", "shard"), None, None, None),
            P("group", None, None, None),
        ),
        check_vma=False,
    )
```

```python
import functools

import jax
import jax.numpy as jnp
from jax import lax
from jax.experimental import pallas as pl
from jax.experimental.pallas import tpu as pltpu
from jax.sharding import PartitionSpec as P

BLK = 512
F32, BF16 = jnp.float32, jnp.bfloat16
ROWS, COLS, HALO = 28, 28, 3
PIX = ROWS * COLS
HROWS = ROWS // 2
XROWS, XCOLS = HROWS + 2 * HALO, COLS + 2 * HALO
NT = (((1,), (1,)), ((), ()))
TN = (((0,), (0,)), ((), ()))


def at8(start, size):
    return pl.ds(pl.multiple_of(start, 8), size)


def put_row(x2, half, row, line):
    for blk in range(4):
        start = (row * XCOLS + HALO) * 8 + half * 4 + blk
        x2[pl.ds(start, COLS, stride=8), :] = line[:, 128 * blk : 128 * blk + 128]


def fill_images(x2, img):
    x2[...] = jnp.zeros_like(x2)

    @pl.loop(0, HROWS + HALO)
    def _(i):
        put_row(x2, 0, i + HALO, img[i].astype(F32))
        put_row(x2, 1, i, img[i + HROWS - HALO].astype(F32))


def conv_row(x2, w2, c2, h, flip):
    for w0 in range(0, COLS, 14):
        acc = jnp.zeros((14, 8, 128), F32)
        for a in range(7):
            row = x2[at8(((h + a) * XCOLS + w0) * 8, 160), :].reshape(20, 8, 128)
            for b in range(7):
                tap = 48 - 7 * a - b if flip else 7 * a + b
                acc = acc + row[b : b + 14] * w2[8 * tap : 8 * tap + 8, :][None]
        c2[at8((h * COLS + w0) * 8, 112), :] = acc.reshape(112, 128)


def norm_rows(c2, xhat, rstd):
    @pl.loop(0, 7)
    def _(k):
        for half in range(2):
            parts = [c2[pl.ds(k * 448 + half * 4 + blk, 56, stride=8), :] for blk in range(4)]
            mean = jnp.sum(parts[0] + parts[1] + parts[2] + parts[3], axis=1, keepdims=True) * (1.0 / 512)
            parts = [v - mean for v in parts]
            sq = [v * v for v in parts]
            var = jnp.sum(sq[0] + sq[1] + sq[2] + sq[3], axis=1, keepdims=True) * (1.0 / 512)
            inv = 1.0 / jnp.sqrt(var + 1e-06)
            rows = at8(half * 392 + k * 56, 56)
            for blk in range(4):
                xhat[rows, 128 * blk : 128 * blk + 128] = parts[blk] * inv
            rstd[rows, :] = jnp.broadcast_to(inv, (56, 128))


def scale_rows(xhat, gain, lhs):
    @pl.loop(0, 7)
    def _(k):
        rows = pl.ds(pl.multiple_of(k * 112, 16), 112)
        lhs[0, rows, :] = (xhat[rows, :] * gain[...]).astype(BF16)


def flat_rows(cot, rhs):
    @pl.loop(0, 7)
    def _(k):
        lines = [cot[4 * k + r].astype(F32) for r in range(4)]
        rhs[4, pl.ds(pl.multiple_of(k * 112, 16), 112), :] = jnp.concatenate(lines, axis=0).astype(BF16)


def gelu_pair(v):
    cdf = 0.5 * (1.0 + lax.erf(v * 0.7071067811865476))
    pdf = 0.3989422804014327 * jnp.exp(-0.5 * v * v)
    return v * cdf, cdf + v * pdf


def up_step(lhs, up, slope, j):
    cols = pl.ds(pl.multiple_of(j * 256, 256), 256)
    part = pl.ds(pl.multiple_of(lax.rem(j, 2) * 256, 256), 256)
    pre = jnp.dot(lhs[0], up[:, cols], preferred_element_type=F32)
    act, der = gelu_pair(pre)
    lhs[1 + lax.div(j, 2), :, part] = act.astype(BF16)
    slope[j] = der


def back_step(rhs, down, slope, j):
    rows = pl.ds(pl.multiple_of(j * 256, 256), 256)
    part = pl.ds(pl.multiple_of(lax.rem(j, 2) * 256, 256), 256)
    back = lax.dot_general(rhs[4], down[rows, :], NT, preferred_element_type=F32)
    rhs[lax.div(j, 2), :, part] = (back * slope[j]).astype(BF16)


def grad_tile(lhs, rhs, k, scale):
    left = jnp.maximum(k - 3, 0)
    right = jnp.minimum(k, 4)
    return lax.dot_general(lhs[left], rhs[right], TN, preferred_element_type=F32) * scale


def branch_cols(lhs, down, out, j):
    cols = pl.ds(pl.multiple_of(j * 256, 256), 256)
    acc = jnp.dot(lhs[1], down[0:512, cols], preferred_element_type=F32)
    for k in range(1, 4):
        acc = acc + jnp.dot(lhs[1 + k], down[512 * k : 512 * k + 512, cols], preferred_element_type=F32)
    out[:, cols] = acc


def back_u_cols(rhs, up, out, j):
    rows = pl.ds(pl.multiple_of(j * 256, 256), 256)
    acc = lax.dot_general(rhs[0], up[rows, 0:512], NT, preferred_element_type=F32)
    for k in range(1, 4):
        acc = acc + lax.dot_general(rhs[k], up[rows, 512 * k : 512 * k + 512], NT, preferred_element_type=F32)
    out[:, rows] = acc


def mix_rows(img, branch, mixed):
    @pl.loop(0, 14)
    def _(k):
        lines = branch[at8(k * 56, 56), :]
        for r in range(2):
            mixed[2 * k + r] = (img[2 * k + r].astype(F32) + lines[28 * r : 28 * r + 28]).astype(BF16)


def norm_back_rows(back, xhat, rstd, gain):
    @pl.loop(0, 14)
    def _(k):
        rows = at8(k * 56, 56)
        grad = back[rows, :] * gain[...]
        unit = xhat[rows, :]
        first = jnp.sum(grad, axis=1, keepdims=True) * (1.0 / 512)
        second = jnp.sum(grad * unit, axis=1, keepdims=True) * (1.0 / 512)
        back[rows, :] = rstd[rows, 0:1] * (grad - first - unit * second)


def fill_back(x2, back):
    @pl.loop(0, 8)
    def _(i):
        lines = back[at8(i * 56, 56), :]
        for r in range(2):
            put_row(x2, 0, 2 * i + r + HALO, lines[28 * r : 28 * r + 28])
        lines = back[at8((i + 6) * 56, 56), :]
        for r in range(2):
            put_row(x2, 1, 2 * i + r + 1, lines[28 * r : 28 * r + 28])

    put_row(x2, 0, 16 + HALO, back[448:476, :])
    put_row(x2, 1, 0, back[308:336, :])


def conv_back_rows(x2, w2, c2, cot, out):
    @pl.loop(0, HROWS)
    def _(h):
        conv_row(x2, w2, c2, h, True)
        for half in range(2):
            line = [c2[pl.ds(h * COLS * 8 + half * 4 + blk, COLS, stride=8), :] for blk in range(4)]
            back = jnp.concatenate(line, axis=1)
            out[half * HROWS + h] = (cot[half * HROWS + h].astype(F32) + back).astype(BF16)


MESH = pl.DeviceIdType.MESH
PAIRS = [(i, j) for i in range(BLK // 128) for j in range(i, BLK // 128)]


def finish_kernel(mixed_in, out_in, packed_in, mixed, out, stat, lines, packed, blocks, into, back):
    load = pltpu.make_async_copy(packed_in, packed, into.at[8])
    load.start()
    loads, stores = [], []
    for k in range(8):
        rows = pl.ds(7 * (k % 4), 7)
        src, dst = (mixed_in, mixed) if k < 4 else (out_in, out)
        loads.append(pltpu.make_async_copy(src.at[rows], lines.at[k], into.at[k]))
        stores.append(pltpu.make_async_copy(lines.at[k], dst.at[rows], back.at[k]))
    for copy in loads:
        copy.start()
    load.wait()
    for side in range(2):
        for b, (i, j) in enumerate(PAIRS):
            part = packed[side, 128 * b : 128 * b + 128, :].astype(F32)
            blocks[side, 128 * i : 128 * i + 128, 128 * j : 128 * j + 128] = part
            if i != j:
                blocks[side, 128 * j : 128 * j + 128, 128 * i : 128 * i + 128] = part.T
        stores.append(pltpu.make_async_copy(blocks.at[side], stat.at[side], back.at[8 + side]))
        stores[-1].start()
        for k in range(4 * side, 4 * side + 4):
            loads[k].wait()
            stores[k].start()
    for copy in stores:
        copy.wait()


def block_kernel(
    n, img_hbm, cot_hbm, dw, gain, up_in, down_in, owner,
    mixed_hbm, out_hbm, ag,
    x2, w2, c2, xhat, rstd, lhs, rhs, up, down, slope, wide, dwb, p, a0, q, a1, gfull, m, c1, img, cot, mixed, out,
    dws, dwr, ups, upr, downs, downr, a0s, a0r, a1s, a1r, gs, gr, cs, cr, ds, dr, es, er, ios,
):
    img_copy = pltpu.make_async_copy(img_hbm, img, ios.at[0])
    cot_copy = pltpu.make_async_copy(cot_hbm, cot, ios.at[1])
    mixed_copy = pltpu.make_async_copy(mixed, mixed_hbm, ios.at[2])
    out_copy = pltpu.make_async_copy(out, out_hbm, ios.at[3])
    img_copy.start()
    cot_copy.start()
    g, s = lax.axis_index("group"), lax.axis_index("shard")
    core, pair = lax.rem(s, 2), lax.div(s, 2)
    sib = s + 1 - 2 * core
    tile = BLK
    half, chunk = tile // 2, len(PAIRS) * 128 // n

    def dma(src, dst, ssem, rsem, group, shard):
        return pltpu.make_async_remote_copy(
            src_ref=src, dst_ref=dst, send_sem=ssem, recv_sem=rsem, device_id=(group, shard), device_id_type=MESH
        )

    def peer(i):
        return 2 * lax.rem(pair + i, n) + core

    def gather(mine, place, send, recv):
        def out_copy(i):
            return dma(mine, place(s), send.at[0, i], recv.at[0, i], g, peer(i))

        def on_copy(i):
            j = peer(n - i)
            return dma(mine if i == 0 else place(j), place(s if i == 0 else j), send.at[1, i], recv.at[1, i], g, sib)

        def start():
            on_copy(0).start()
            for i in range(1, n):
                out_copy(i).start()

        def forward():
            for i in range(1, n):
                out_copy(i).wait_recv()
                on_copy(i).start()

        def arrived():
            for i in range(n):
                on_copy(i).wait_recv()

        def finish():
            on_copy(0).wait_send()
            for i in range(1, n):
                out_copy(i).wait_send()
                on_copy(i).wait_send()

        return start, forward, arrived, finish

    zpos, ypos = lax.div(pair, 2), lax.rem(pair, 2)
    across = s + 2 - 4 * ypos
    beyond = g + 1 - 2 * lax.rem(g, 2)

    def spread(place, send, recv):
        def block(i, y):
            return 4 * lax.rem(zpos + 4 - i, 4) + 2 * y + core

        def z_copy(i):
            return dma(place(s), place(s), send.at[0, i], recv.at[0, i], g, 4 * lax.rem(zpos + i, 4) + 2 * ypos + core)

        def y_copy(i, h):
            ref = place(block(i, ypos), h)
            return dma(ref, ref, send.at[1 + h, i], recv.at[1 + h, i], beyond if h else g, across)

        def core_z(i):
            ref = place(block(i, ypos))
            return dma(ref, ref, send.at[3, i], recv.at[3, i], g, sib)

        def core_y(i, h):
            ref = place(block(i, 1 - ypos), h)
            return dma(ref, ref, send.at[4 + h, i], recv.at[4 + h, i], g, sib)

        def start():
            for i in range(1, 4):
                z_copy(i).start()
            y_copy(0, 0).start()
            y_copy(0, 1).start()
            core_z(0).start()

        def relay_z(i):
            z_copy(i).wait_recv()
            y_copy(i, 0).start()
            y_copy(i, 1).start()
            core_z(i).start()

        def relay_y(i):
            for h in range(2):
                y_copy(i, h).wait_recv()
                core_y(i, h).start()

        def arrived():
            for i in range(4):
                core_z(i).wait_recv()
                core_y(i, 0).wait_recv()
                core_y(i, 1).wait_recv()

        def finish():
            for i in range(4):
                if i:
                    z_copy(i).wait_send()
                core_z(i).wait_send()
                for h in range(2):
                    y_copy(i, h).wait_send()
                    core_y(i, h).wait_send()

        return start, relay_z, relay_y, arrived, finish

    target = (pair, 2 * lax.rem(g + 1, n) + core)
    source = (lax.rem(pair + n - 1, n), 2 * g + core)
    barrier = pltpu.get_barrier_semaphore()

    def greet(group, shard):
        pl.semaphore_signal(barrier, inc=1, device_id=(group, shard), device_id_type=MESH)

    for i in range(1, 2 * n):
        greet(g, lax.rem(s + i, 2 * n))
    for i in range(1, n):
        greet(lax.rem(g + i, n), s)
    greet(*target)
    greet(*source)
    greet(beyond, across)

    taps = dw[...].astype(F32).T
    taps = jnp.concatenate([taps, taps, taps, taps], axis=1)
    lane = lax.broadcasted_iota(jnp.int32, taps.shape, 1)
    low = 32 * lax.rem(s, 4)
    taps = jnp.where((lane >= low) & (lane < low + 32), taps, 0.0)
    dwb[s] = jnp.zeros((64, 128), BF16)
    dwb[s, 0:49, :] = taps.astype(BF16)
    up[pl.ds(pl.multiple_of(s * 32, 32), 32), :] = up_in[...]
    down[pl.ds(pl.multiple_of(s * 128, 128), 128), :] = down_in[...]
    img_copy.wait()
    fill_images(x2, img)

    def up_place(j, h=None):
        return up.at[pl.ds(pl.multiple_of(j * 32 + (h or 0) * 16, 16), 32 if h is None else 16)]

    def down_place(j, h=None):
        return down.at[pl.ds(pl.multiple_of(j * 128 + (h or 0) * 64, 64), 128 if h is None else 64)]

    up_start, up_relay_z, up_relay_y, up_arrived, up_finish = spread(up_place, ups, upr)
    down_start, down_relay_z, down_relay_y, down_arrived, down_finish = spread(down_place, downs, downr)

    def ag_place(j):
        start = lax.rem(lax.div(j, 2) + n - 1, n) * chunk
        return ag.at[lax.rem(j, 2), pl.ds(pl.multiple_of(start, chunk), chunk)]

    ag_start, ag_forward, ag_arrived, ag_finish = gather(ag_place(s), ag_place, es, er)

    def dw_copy(i):
        return dma(dwb.at[s], dwb.at[s], dws.at[i], dwr.at[i], g, lax.rem(s + i, 2 * n))

    pl.semaphore_wait(barrier, 3 * n + 1)
    for i in range(1, 2 * n):
        dw_copy(i).start()
    up_start()
    cot_copy.wait()
    flat_rows(cot, rhs)
    for i in range(1, 2 * n):
        dw_copy(i).wait_recv()
    for blk in range(4):
        lines = [dwb[4 * blk + t].astype(F32) for t in range(4)]
        line = lines[0] + lines[1] + lines[2] + lines[3]
        w2[pl.ds(blk, 64, stride=8), :] = line
        w2[pl.ds(blk + 4, 64, stride=8), :] = line

    def conv_rows(lo, hi):
        @pl.loop(lo, hi)
        def _(h):
            conv_row(x2, w2, c2, h, False)

    conv_rows(0, 5)
    up_relay_z(1)
    up_relay_z(3)
    conv_rows(5, 9)
    up_relay_z(2)
    down_start()
    conv_rows(9, HROWS)
    up_relay_y(0)
    up_relay_y(1)
    up_relay_y(3)
    norm_rows(c2, xhat, rstd)
    scale_rows(xhat, gain, lhs)
    up_relay_y(2)
    up_arrived()

    def up_steps(lo, hi):
        @pl.loop(lo, hi)
        def _(j):
            up_step(lhs, up, slope, j)

    up_steps(0, 2)
    down_relay_z(1)
    down_relay_z(3)
    up_steps(2, 4)
    down_relay_z(2)
    down_relay_y(0)
    up_steps(4, 7)
    down_relay_y(1)
    down_relay_y(3)
    up_steps(7, 8)
    down_relay_y(2)
    down_arrived()

    @pl.loop(0, 8)
    def _(j):
        back_step(rhs, down, slope, j)

    own = pl.ds(pl.multiple_of(core * half, half), half)
    other = pl.ds(pl.multiple_of((1 - core) * half, half), half)
    scale = (2 * n * PIX) ** -0.5

    def slot(i):
        return lax.rem(pair + 1 + i, n)

    def a0_copy(i):
        return dma(p.at[i, other], a0.at[i], a0s.at[i], a0r.at[i], g, sib)

    def a1_copy(i):
        return dma(q.at[i], a1.at[i], a1s.at[i], a1r.at[i], g, 2 * slot(i) + core)

    def pass_on(i):
        a0_copy(i).wait_recv()
        q[i] = (p[i, own].astype(F32) + a0[i].astype(F32)).astype(BF16)
        a1_copy(i).start()

    @pl.loop(0, n)
    def _(i):
        p[i] = grad_tile(lhs, rhs, owner[slot(i)], scale).astype(BF16)
        a0_copy(i).start()

        @pl.when(i > 0)
        def _():
            pass_on(i - 1)

    @pl.loop(0, 2)
    def _(j):
        branch_cols(lhs, down, wide, j)

    mix_rows(img, wide, mixed)
    mixed_copy.start()

    @pl.loop(0, 2)
    def _(j):
        back_u_cols(rhs, up, wide, j)

    norm_back_rows(wide, xhat, rstd, gain)
    fill_back(x2, wide)
    conv_back_rows(x2, w2, c2, cot, out)
    out_copy.start()

    a0_copy(n - 1).wait_recv()
    acc = p[n - 1, own].astype(F32) + a0[n - 1].astype(F32)
    for i in range(n - 1):
        a1_copy(i).wait_recv()
        acc = acc + a1[i].astype(F32)
    gfull[own] = acc.astype(BF16)
    g_copy = dma(gfull.at[own], gfull.at[own], gs, gr, g, sib)
    g_copy.start()
    g_copy.wait_recv()
    whole = gfull[...]
    side = jnp.where(core == 0, whole, whole.T)
    stat = lax.dot_general(side, side, NT, preferred_element_type=F32)
    stat = (stat * (1.0 / tile)).astype(BF16)
    for b, (i, j) in enumerate(PAIRS):
        m[128 * b : 128 * b + 128, :] = stat[128 * i : 128 * i + 128, 128 * j : 128 * j + 128]

    def m_chunk(j):
        return pl.ds(pl.multiple_of(j * chunk, chunk), chunk)

    def c_copy(i):
        j = lax.rem(g + i, n)
        return dma(m.at[m_chunk(j)], c1.at[i], cs.at[i], cr.at[i], j, s)

    for i in range(1, n):
        c_copy(i).start()
    acc = m[m_chunk(g), :].astype(F32)
    for i in range(1, n):
        c_copy(i).wait_recv()
        acc = acc + c1[i].astype(F32)
    c1[0] = acc.astype(BF16)
    d_copy = dma(c1.at[0], ag_place(target[1]), ds, dr, *target)
    d_copy.start()
    d_copy.wait_recv()
    ag_start()
    ag_forward()
    ag_arrived()
    mixed_copy.wait()
    out_copy.wait()
    up_finish()
    down_finish()
    ag_finish()
    for i in range(1, 2 * n):
        dw_copy(i).wait_send()
    for i in range(n):
        a0_copy(i).wait_send()
    for i in range(n - 1):
        a1_copy(i).wait_send()
        c_copy(i + 1).wait_send()
    g_copy.wait_send()
    d_copy.wait_send()


def local(images, cotangent, dw_kernel, norm_gain, w_up, w_down, owner_table):
    n = lax.axis_size("group")
    half, chunk = BLK // 2, len(PAIRS) * 128 // n
    sem = pltpu.SemaphoreType.DMA
    vmem = pltpu.VMEM
    width = images.shape[-1]
    mixed, back, packed = pl.pallas_call(
        functools.partial(block_kernel, n),
        out_shape=(
            jax.ShapeDtypeStruct((ROWS, COLS, width), BF16),
            jax.ShapeDtypeStruct((ROWS, COLS, width), BF16),
            jax.ShapeDtypeStruct((2, n * chunk, 128), BF16),
        ),
        in_specs=[pl.BlockSpec(memory_space=pl.ANY)] * 2 + [pl.BlockSpec(memory_space=vmem)] * 4 + [pl.BlockSpec(memory_space=pltpu.SMEM)],
        out_specs=[pl.BlockSpec(memory_space=pl.ANY)] * 2 + [pl.BlockSpec(memory_space=vmem)],
        scratch_shapes=[
            vmem((XROWS * XCOLS * 8, 128), F32),
            vmem((512, 128), F32),
            vmem((HROWS * COLS * 8, 128), F32),
            vmem((PIX, width), F32),
            vmem((PIX, 128), F32),
            vmem((5, PIX, width), BF16),
            vmem((5, PIX, width), BF16),
            vmem((512, 2048), BF16),
            vmem((2048, 512), BF16),
            vmem((8, PIX, 256), F32),
            vmem((PIX, width), F32),
            vmem((2 * n, 64, 128), BF16),
            vmem((n, BLK, BLK), BF16),
            vmem((n, half, BLK), BF16),
            vmem((n - 1, half, BLK), BF16),
            vmem((n - 1, half, BLK), BF16),
            vmem((BLK, BLK), BF16),
            vmem((n * chunk, 128), BF16),
            vmem((n, chunk, 128), BF16),
            vmem((ROWS, COLS, width), BF16),
            vmem((ROWS, COLS, width), BF16),
            vmem((ROWS, COLS, width), BF16),
            vmem((ROWS, COLS, width), BF16),
            sem((2 * n,)), sem((2 * n,)),
            sem((6, 4)), sem((6, 4)),
            sem((6, 4)), sem((6, 4)),
            sem((n,)), sem((n,)),
            sem((n - 1,)), sem((n - 1,)),
            sem, sem,
            sem((n,)), sem((n,)),
            sem, sem,
            sem((2, n)), sem((2, n)),
            sem((4,)),
        ],
        compiler_params=pltpu.CompilerParams(collective_id=0, has_side_effects=True, vmem_limit_bytes=60 * 2**20),
    )(images[0], cotangent[0], dw_kernel.T, norm_gain.reshape(1, width), w_up, w_down, owner_table)
    mixed, back, stat = pl.pallas_call(
        finish_kernel,
        out_shape=(
            jax.ShapeDtypeStruct((ROWS, COLS, width), BF16),
            jax.ShapeDtypeStruct((ROWS, COLS, width), BF16),
            jax.ShapeDtypeStruct((2, BLK, BLK), F32),
        ),
        in_specs=[pl.BlockSpec(memory_space=pl.ANY)] * 3,
        out_specs=[pl.BlockSpec(memory_space=pl.ANY)] * 3,
        scratch_shapes=[
            vmem((8, 7, COLS, width), BF16),
            vmem((2, n * chunk, 128), BF16),
            vmem((2, BLK, BLK), F32),
            sem((9,)), sem((10,)),
        ],
        compiler_params=pltpu.CompilerParams(vmem_limit_bytes=60 * 2**20),
    )(mixed, back, packed)
    return (mixed[None], back[None], stat[None])


def solution(mesh):
    return jax.shard_map(
        local,
        mesh=mesh,
        in_specs=(
            P(("group", "shard"), None, None, None),
            P(("group", "shard"), None, None, None),
            P(None, "shard"),
            P(),
            P("shard", None),
            P("shard", None),
            P(),
        ),
        out_specs=(
            P(("group", "shard"), None, None, None),
            P(("group", "shard"), None, None, None),
            P("group", None, None, None),
        ),
        check_vma=False,
    )
```

```python
import functools

import jax
import jax.numpy as jnp
from jax import lax
from jax.experimental import pallas as pl
from jax.experimental.pallas import tpu as pltpu
from jax.sharding import PartitionSpec as P

BLK = 512
F32, BF16 = jnp.float32, jnp.bfloat16
ROWS, COLS, HALO = 28, 28, 3
PIX = ROWS * COLS
HROWS = ROWS // 2
XROWS, XCOLS = HROWS + 2 * HALO, COLS + 2 * HALO
NT = (((1,), (1,)), ((), ()))
TN = (((0,), (0,)), ((), ()))


def at8(start, size):
    return pl.ds(pl.multiple_of(start, 8), size)


def put_row(x2, half, row, line):
    for blk in range(4):
        start = (row * XCOLS + HALO) * 8 + half * 4 + blk
        x2[pl.ds(start, COLS, stride=8), :] = line[:, 128 * blk : 128 * blk + 128]


def fill_images(x2, img):
    x2[...] = jnp.zeros_like(x2)

    @pl.loop(0, HROWS + HALO)
    def _(i):
        put_row(x2, 0, i + HALO, img[i].astype(F32))
        put_row(x2, 1, i, img[i + HROWS - HALO].astype(F32))


def conv_row(x2, w2, c2, h, flip):
    for w0 in range(0, COLS, 14):
        acc = jnp.zeros((14, 8, 128), F32)
        for a in range(7):
            row = x2[at8(((h + a) * XCOLS + w0) * 8, 160), :].reshape(20, 8, 128)
            for b in range(7):
                tap = 48 - 7 * a - b if flip else 7 * a + b
                acc = acc + row[b : b + 14] * w2[8 * tap : 8 * tap + 8, :][None]
        c2[at8((h * COLS + w0) * 8, 112), :] = acc.reshape(112, 128)


def norm_rows(c2, xhat, rstd, lo, hi):
    @pl.loop(lo, hi)
    def _(k):
        for half in range(2):
            parts = [c2[pl.ds(k * 448 + half * 4 + blk, 56, stride=8), :] for blk in range(4)]
            mean = jnp.sum(parts[0] + parts[1] + parts[2] + parts[3], axis=1, keepdims=True) * (1.0 / 512)
            parts = [v - mean for v in parts]
            sq = [v * v for v in parts]
            var = jnp.sum(sq[0] + sq[1] + sq[2] + sq[3], axis=1, keepdims=True) * (1.0 / 512)
            inv = 1.0 / jnp.sqrt(var + 1e-06)
            rows = at8(half * 392 + k * 56, 56)
            for blk in range(4):
                xhat[rows, 128 * blk : 128 * blk + 128] = parts[blk] * inv
            rstd[rows, :] = jnp.broadcast_to(inv, (56, 128))


def scale_rows(xhat, gain, lhs):
    @pl.loop(0, 7)
    def _(k):
        rows = pl.ds(pl.multiple_of(k * 112, 16), 112)
        lhs[0, rows, :] = (xhat[rows, :] * gain[...]).astype(BF16)


def flat_rows(cot, rhs):
    @pl.loop(0, 7)
    def _(k):
        lines = [cot[4 * k + r].astype(F32) for r in range(4)]
        rhs[4, pl.ds(pl.multiple_of(k * 112, 16), 112), :] = jnp.concatenate(lines, axis=0).astype(BF16)


def gelu_pair(v):
    cdf = 0.5 * (1.0 + lax.erf(v * 0.7071067811865476))
    pdf = 0.3989422804014327 * jnp.exp(-0.5 * v * v)
    return v * cdf, cdf + v * pdf


def up_step(lhs, up, slope, j):
    cols = pl.ds(pl.multiple_of(j * 256, 256), 256)
    part = pl.ds(pl.multiple_of(lax.rem(j, 2) * 256, 256), 256)
    pre = jnp.dot(lhs[0], up[:, cols], preferred_element_type=F32)
    act, der = gelu_pair(pre)
    lhs[1 + lax.div(j, 2), :, part] = act.astype(BF16)
    slope[j] = der


def back_step(rhs, down, slope, j):
    rows = pl.ds(pl.multiple_of(j * 256, 256), 256)
    part = pl.ds(pl.multiple_of(lax.rem(j, 2) * 256, 256), 256)
    back = lax.dot_general(rhs[4], down[rows, :], NT, preferred_element_type=F32)
    rhs[lax.div(j, 2), :, part] = (back * slope[j]).astype(BF16)


def grad_tile(lhs, rhs, k, scale):
    left = jnp.maximum(k - 3, 0)
    right = jnp.minimum(k, 4)
    return lax.dot_general(lhs[left], rhs[right], TN, preferred_element_type=F32) * scale


def branch_cols(lhs, down, out, j):
    cols = pl.ds(pl.multiple_of(j * 256, 256), 256)
    acc = jnp.dot(lhs[1], down[0:512, cols], preferred_element_type=F32)
    for k in range(1, 4):
        acc = acc + jnp.dot(lhs[1 + k], down[512 * k : 512 * k + 512, cols], preferred_element_type=F32)
    out[:, cols] = acc


def back_u_cols(rhs, up, out, j):
    rows = pl.ds(pl.multiple_of(j * 256, 256), 256)
    acc = lax.dot_general(rhs[0], up[rows, 0:512], NT, preferred_element_type=F32)
    for k in range(1, 4):
        acc = acc + lax.dot_general(rhs[k], up[rows, 512 * k : 512 * k + 512], NT, preferred_element_type=F32)
    out[:, rows] = acc


def mix_rows(img, branch, mixed):
    @pl.loop(0, 14)
    def _(k):
        lines = branch[at8(k * 56, 56), :]
        for r in range(2):
            mixed[2 * k + r] = (img[2 * k + r].astype(F32) + lines[28 * r : 28 * r + 28]).astype(BF16)


def norm_back_rows(back, xhat, rstd, gain):
    @pl.loop(0, 14)
    def _(k):
        rows = at8(k * 56, 56)
        grad = back[rows, :] * gain[...]
        unit = xhat[rows, :]
        first = jnp.sum(grad, axis=1, keepdims=True) * (1.0 / 512)
        second = jnp.sum(grad * unit, axis=1, keepdims=True) * (1.0 / 512)
        back[rows, :] = rstd[rows, 0:1] * (grad - first - unit * second)


def fill_back(x2, back):
    @pl.loop(0, 8)
    def _(i):
        lines = back[at8(i * 56, 56), :]
        for r in range(2):
            put_row(x2, 0, 2 * i + r + HALO, lines[28 * r : 28 * r + 28])
        lines = back[at8((i + 6) * 56, 56), :]
        for r in range(2):
            put_row(x2, 1, 2 * i + r + 1, lines[28 * r : 28 * r + 28])

    put_row(x2, 0, 16 + HALO, back[448:476, :])
    put_row(x2, 1, 0, back[308:336, :])


def conv_back_rows(x2, w2, c2, cot, out):
    @pl.loop(0, HROWS)
    def _(h):
        conv_row(x2, w2, c2, h, True)
        for half in range(2):
            line = [c2[pl.ds(h * COLS * 8 + half * 4 + blk, COLS, stride=8), :] for blk in range(4)]
            back = jnp.concatenate(line, axis=1)
            out[half * HROWS + h] = (cot[half * HROWS + h].astype(F32) + back).astype(BF16)


MESH = pl.DeviceIdType.MESH
PAIRS = [(i, j) for i in range(BLK // 128) for j in range(i, BLK // 128)]


def finish_kernel(mixed_in, out_in, packed_in, mixed, out, stat, lines, packed, blocks, into, back):
    load = pltpu.make_async_copy(packed_in, packed, into.at[8])
    load.start()
    loads, stores = [], []
    for k in range(8):
        rows = pl.ds(7 * (k % 4), 7)
        src, dst = (mixed_in, mixed) if k < 4 else (out_in, out)
        loads.append(pltpu.make_async_copy(src.at[rows], lines.at[k], into.at[k]))
        stores.append(pltpu.make_async_copy(lines.at[k], dst.at[rows], back.at[k]))
    for copy in loads:
        copy.start()
    load.wait()
    for side in range(2):
        for b, (i, j) in enumerate(PAIRS):
            part = packed[side, 128 * b : 128 * b + 128, :].astype(F32)
            blocks[side, 128 * i : 128 * i + 128, 128 * j : 128 * j + 128] = part
            if i != j:
                blocks[side, 128 * j : 128 * j + 128, 128 * i : 128 * i + 128] = part.T
        stores.append(pltpu.make_async_copy(blocks.at[side], stat.at[side], back.at[8 + side]))
        stores[-1].start()
        for k in range(4 * side, 4 * side + 4):
            loads[k].wait()
            stores[k].start()
    for copy in stores:
        copy.wait()


def block_kernel(
    n, img_hbm, cot_hbm, dw, gain, up_in, down_in, owner,
    mixed_hbm, out_hbm, ag,
    x2, w2, c2, xhat, rstd, lhs, rhs, up, down, slope, wide, dwb, flat, p, a0, q, a1, gfull, m, c1, img, cot, mixed, out,
    dws, dwr, ups, upr, downs, downr, a0s, a0r, a1s, a1r, gs, gr, cs, cr, ds, dr, es, er, ios,
):
    img_copy = pltpu.make_async_copy(img_hbm, img, ios.at[0])
    cot_copy = pltpu.make_async_copy(cot_hbm, cot, ios.at[1])
    mixed_copy = pltpu.make_async_copy(mixed, mixed_hbm, ios.at[2])
    out_copy = pltpu.make_async_copy(out, out_hbm, ios.at[3])
    img_copy.start()
    cot_copy.start()
    g, s = lax.axis_index("group"), lax.axis_index("shard")
    core, pair = lax.rem(s, 2), lax.div(s, 2)
    sib = s + 1 - 2 * core
    tile = BLK
    half, chunk = tile // 2, len(PAIRS) * 128 // n

    def dma(src, dst, ssem, rsem, group, shard):
        return pltpu.make_async_remote_copy(
            src_ref=src, dst_ref=dst, send_sem=ssem, recv_sem=rsem, device_id=(group, shard), device_id_type=MESH
        )

    def peer(i):
        return 2 * lax.rem(pair + i, n) + core

    def gather(mine, place, send, recv):
        def out_copy(i):
            return dma(mine, place(s), send.at[0, i], recv.at[0, i], g, peer(i))

        def on_copy(i):
            j = peer(n - i)
            return dma(mine if i == 0 else place(j), place(s if i == 0 else j), send.at[1, i], recv.at[1, i], g, sib)

        def start():
            on_copy(0).start()
            for i in range(1, n):
                out_copy(i).start()

        def forward():
            for i in range(1, n):
                out_copy(i).wait_recv()
                on_copy(i).start()

        def arrived():
            for i in range(n):
                on_copy(i).wait_recv()

        def finish():
            on_copy(0).wait_send()
            for i in range(1, n):
                out_copy(i).wait_send()
                on_copy(i).wait_send()

        return start, forward, arrived, finish

    zpos, ypos = lax.div(pair, 2), lax.rem(pair, 2)
    across = s + 2 - 4 * ypos
    beyond = g + 1 - 2 * lax.rem(g, 2)

    def spread(place, send, recv):
        def block(i, y):
            return 4 * lax.rem(zpos + 4 - i, 4) + 2 * y + core

        def z_copy(i):
            return dma(place(s), place(s), send.at[0, i], recv.at[0, i], g, 4 * lax.rem(zpos + i, 4) + 2 * ypos + core)

        def y_copy(i, h):
            ref = place(block(i, ypos), h)
            return dma(ref, ref, send.at[1 + h, i], recv.at[1 + h, i], beyond if h else g, across)

        def core_z(i):
            ref = place(block(i, ypos))
            return dma(ref, ref, send.at[3, i], recv.at[3, i], g, sib)

        def core_y(i, h):
            ref = place(block(i, 1 - ypos), h)
            return dma(ref, ref, send.at[4 + h, i], recv.at[4 + h, i], g, sib)

        def start():
            z_copy(1).start()
            z_copy(3).start()
            y_copy(0, 0).start()
            y_copy(0, 1).start()
            core_z(0).start()

        def start_far():
            z_copy(2).start()

        def relay_z(i):
            z_copy(i).wait_recv()
            y_copy(i, 0).start()
            y_copy(i, 1).start()
            core_z(i).start()

        def relay_y(i):
            for h in range(2):
                y_copy(i, h).wait_recv()
                core_y(i, h).start()

        def arrived():
            for i in range(4):
                core_z(i).wait_recv()
                core_y(i, 0).wait_recv()
                core_y(i, 1).wait_recv()

        def finish():
            for i in range(4):
                if i:
                    z_copy(i).wait_send()
                core_z(i).wait_send()
                for h in range(2):
                    y_copy(i, h).wait_send()
                    core_y(i, h).wait_send()

        return start, start_far, relay_z, relay_y, arrived, finish

    mirror = (pair, 2 * g + core)
    barrier = pltpu.get_barrier_semaphore()

    def greet(group, shard):
        pl.semaphore_signal(barrier, inc=1, device_id=(group, shard), device_id_type=MESH)

    for i in range(1, 2 * n):
        greet(g, lax.rem(s + i, 2 * n))
    for i in range(1, n):
        greet(lax.rem(g + i, n), s)

    @pl.when(pair != g)
    def _():
        greet(*mirror)

    greet(beyond, across)

    flat[...] = jnp.zeros_like(flat)
    flat[0:49, :] = dw[...].astype(F32).T
    dwb[s] = jnp.concatenate([flat[16 * t : 16 * t + 16, :] for t in range(4)], axis=1).astype(BF16)
    up[pl.ds(pl.multiple_of(s * 32, 32), 32), :] = up_in[...]
    down[pl.ds(pl.multiple_of(s * 128, 128), 128), :] = down_in[...]
    img_copy.wait()
    fill_images(x2, img)

    def up_place(j, h=None):
        return up.at[pl.ds(pl.multiple_of(j * 32 + (h or 0) * 16, 16), 32 if h is None else 16)]

    def down_place(j, h=None):
        return down.at[pl.ds(pl.multiple_of(j * 128 + (h or 0) * 64, 64), 128 if h is None else 64)]

    up_start, up_far, up_relay_z, up_relay_y, up_arrived, up_finish = spread(up_place, ups, upr)
    down_start, down_far, down_relay_z, down_relay_y, down_arrived, down_finish = spread(down_place, downs, downr)

    def ag_place(j):
        start = lax.div(j, 2) * chunk
        return ag.at[lax.rem(j, 2), pl.ds(pl.multiple_of(start, chunk), chunk)]

    ag_start, ag_forward, ag_arrived, ag_finish = gather(ag_place(s), ag_place, es, er)

    def dw_copy(i):
        return dma(dwb.at[s], dwb.at[s], dws.at[i], dwr.at[i], g, lax.rem(s + i, 2 * n))

    pl.semaphore_wait(barrier, 3 * n - jnp.where(pair == g, 1, 0))
    for i in range(1, 2 * n):
        dw_copy(i).start()
    up_start()
    cot_copy.wait()
    flat_rows(cot, rhs)
    for i in range(1, 2 * n):
        dw_copy(i).wait_recv()
    lane = lax.broadcasted_iota(jnp.int32, (16, 128), 1)
    for blk in range(4):
        lines = [dwb[4 * blk + t].astype(F32) for t in range(4)]
        for k in range(4):
            line = jnp.zeros((16, 128), F32)
            for t in range(4):
                moved = lines[t] if t == k else pltpu.roll(lines[t], 32 * ((t - k) % 4), 1)
                line = jnp.where((lane >= 32 * t) & (lane < 32 * t + 32), moved, line)
            w2[pl.ds(128 * k + blk, 16, stride=8), :] = line
            w2[pl.ds(128 * k + blk + 4, 16, stride=8), :] = line

    def conv_rows(lo, hi):
        @pl.loop(lo, hi)
        def _(h):
            conv_row(x2, w2, c2, h, False)

    up_far()
    conv_rows(0, 3)
    up_relay_z(1)
    up_relay_z(3)
    conv_rows(3, 6)
    down_start()
    conv_rows(6, 9)
    up_relay_z(2)
    conv_rows(9, 12)
    up_relay_y(0)
    up_relay_y(1)
    up_relay_y(3)
    down_far()
    conv_rows(12, HROWS)
    norm_rows(c2, xhat, rstd, 0, 4)
    up_relay_y(2)
    down_relay_z(1)
    down_relay_z(3)
    norm_rows(c2, xhat, rstd, 4, 7)
    scale_rows(xhat, gain, lhs)
    up_arrived()

    def up_steps(lo, hi):
        @pl.loop(lo, hi)
        def _(j):
            up_step(lhs, up, slope, j)

    up_steps(0, 2)
    down_relay_z(2)
    up_steps(2, 6)
    down_relay_y(0)
    down_relay_y(1)
    down_relay_y(3)
    up_steps(6, 8)
    down_relay_y(2)
    down_arrived()

    @pl.loop(0, 8)
    def _(j):
        back_step(rhs, down, slope, j)

    own = pl.ds(pl.multiple_of(core * half, half), half)
    other = pl.ds(pl.multiple_of((1 - core) * half, half), half)
    scale = (2 * n * PIX) ** -0.5

    def slot(i):
        return lax.rem(pair + 1 + i, n)

    def a0_copy(i):
        return dma(p.at[i, other], a0.at[i], a0s.at[i], a0r.at[i], g, sib)

    def a1_copy(i):
        return dma(q.at[i], a1.at[i], a1s.at[i], a1r.at[i], g, 2 * slot(i) + core)

    def pass_on(i):
        a0_copy(i).wait_recv()
        q[i] = (p[i, own].astype(F32) + a0[i].astype(F32)).astype(BF16)
        a1_copy(i).start()

    @pl.loop(0, n)
    def _(i):
        p[i] = grad_tile(lhs, rhs, owner[slot(i)], scale).astype(BF16)
        a0_copy(i).start()

        @pl.when(i > 0)
        def _():
            pass_on(i - 1)

    @pl.loop(0, 2)
    def _(j):
        branch_cols(lhs, down, wide, j)

    mix_rows(img, wide, mixed)
    mixed_copy.start()

    @pl.loop(0, 2)
    def _(j):
        back_u_cols(rhs, up, wide, j)

    norm_back_rows(wide, xhat, rstd, gain)
    fill_back(x2, wide)
    conv_back_rows(x2, w2, c2, cot, out)
    out_copy.start()

    a0_copy(n - 1).wait_recv()
    acc = p[n - 1, own].astype(F32) + a0[n - 1].astype(F32)
    for i in range(n - 1):
        a1_copy(i).wait_recv()
        acc = acc + a1[i].astype(F32)
    gfull[own] = acc.astype(BF16)
    g_copy = dma(gfull.at[own], gfull.at[own], gs, gr, g, sib)
    g_copy.start()
    g_copy.wait_recv()
    whole = gfull[...]
    side = jnp.where(core == 0, whole, whole.T)
    stat = lax.dot_general(side, side, NT, preferred_element_type=F32)
    stat = (stat * (1.0 / tile)).astype(BF16)
    for b, (i, j) in enumerate(PAIRS):
        m[128 * b : 128 * b + 128, :] = stat[128 * i : 128 * i + 128, 128 * j : 128 * j + 128]

    def m_chunk(j):
        return pl.ds(pl.multiple_of(j * chunk, chunk), chunk)

    def c_copy(i):
        j = lax.rem(g + i, n)
        return dma(m.at[m_chunk(j)], c1.at[i], cs.at[i], cr.at[i], j, s)

    for i in range(1, n):
        c_copy(i).start()
    acc = m[m_chunk(g), :].astype(F32)
    for i in range(1, n):
        c_copy(i).wait_recv()
        acc = acc + c1[i].astype(F32)
    c1[0] = acc.astype(BF16)
    d_copy = dma(c1.at[0], ag_place(mirror[1]), ds, dr, *mirror)

    @pl.when(pair != g)
    def _():
        d_copy.start()
        d_copy.wait_recv()

    @pl.when(pair == g)
    def _():
        ag[core, m_chunk(g), :] = c1[0]

    ag_start()
    ag_forward()
    ag_arrived()
    mixed_copy.wait()
    out_copy.wait()
    up_finish()
    down_finish()
    ag_finish()
    for i in range(1, 2 * n):
        dw_copy(i).wait_send()
    for i in range(n):
        a0_copy(i).wait_send()
    for i in range(n - 1):
        a1_copy(i).wait_send()
        c_copy(i + 1).wait_send()
    g_copy.wait_send()

    @pl.when(pair != g)
    def _():
        d_copy.wait_send()


def local(images, cotangent, dw_kernel, norm_gain, w_up, w_down, owner_table):
    n = lax.axis_size("group")
    half, chunk = BLK // 2, len(PAIRS) * 128 // n
    sem = pltpu.SemaphoreType.DMA
    vmem = pltpu.VMEM
    width = images.shape[-1]
    mixed, back, packed = pl.pallas_call(
        functools.partial(block_kernel, n),
        out_shape=(
            jax.ShapeDtypeStruct((ROWS, COLS, width), BF16),
            jax.ShapeDtypeStruct((ROWS, COLS, width), BF16),
            jax.ShapeDtypeStruct((2, n * chunk, 128), BF16),
        ),
        in_specs=[pl.BlockSpec(memory_space=pl.ANY)] * 2 + [pl.BlockSpec(memory_space=vmem)] * 4 + [pl.BlockSpec(memory_space=pltpu.SMEM)],
        out_specs=[pl.BlockSpec(memory_space=pl.ANY)] * 2 + [pl.BlockSpec(memory_space=vmem)],
        scratch_shapes=[
            vmem((XROWS * XCOLS * 8, 128), F32),
            vmem((512, 128), F32),
            vmem((HROWS * COLS * 8, 128), F32),
            vmem((PIX, width), F32),
            vmem((PIX, 128), F32),
            vmem((5, PIX, width), BF16),
            vmem((5, PIX, width), BF16),
            vmem((512, 2048), BF16),
            vmem((2048, 512), BF16),
            vmem((8, PIX, 256), F32),
            vmem((PIX, width), F32),
            vmem((2 * n, 16, 128), BF16),
            vmem((64, 32), F32),
            vmem((n, BLK, BLK), BF16),
            vmem((n, half, BLK), BF16),
            vmem((n - 1, half, BLK), BF16),
            vmem((n - 1, half, BLK), BF16),
            vmem((BLK, BLK), BF16),
            vmem((n * chunk, 128), BF16),
            vmem((n, chunk, 128), BF16),
            vmem((ROWS, COLS, width), BF16),
            vmem((ROWS, COLS, width), BF16),
            vmem((ROWS, COLS, width), BF16),
            vmem((ROWS, COLS, width), BF16),
            sem((2 * n,)), sem((2 * n,)),
            sem((6, 4)), sem((6, 4)),
            sem((6, 4)), sem((6, 4)),
            sem((n,)), sem((n,)),
            sem((n - 1,)), sem((n - 1,)),
            sem, sem,
            sem((n,)), sem((n,)),
            sem, sem,
            sem((2, n)), sem((2, n)),
            sem((4,)),
        ],
        compiler_params=pltpu.CompilerParams(collective_id=0, has_side_effects=True, vmem_limit_bytes=60 * 2**20),
    )(images[0], cotangent[0], dw_kernel.T, norm_gain.reshape(1, width), w_up, w_down, owner_table)
    mixed, back, stat = pl.pallas_call(
        finish_kernel,
        out_shape=(
            jax.ShapeDtypeStruct((ROWS, COLS, width), BF16),
            jax.ShapeDtypeStruct((ROWS, COLS, width), BF16),
            jax.ShapeDtypeStruct((2, BLK, BLK), F32),
        ),
        in_specs=[pl.BlockSpec(memory_space=pl.ANY)] * 3,
        out_specs=[pl.BlockSpec(memory_space=pl.ANY)] * 3,
        scratch_shapes=[
            vmem((8, 7, COLS, width), BF16),
            vmem((2, n * chunk, 128), BF16),
            vmem((2, BLK, BLK), F32),
            sem((9,)), sem((10,)),
        ],
        compiler_params=pltpu.CompilerParams(vmem_limit_bytes=60 * 2**20),
    )(mixed, back, packed)
    return (mixed[None], back[None], stat[None])


def solution(mesh):
    return jax.shard_map(
        local,
        mesh=mesh,
        in_specs=(
            P(("group", "shard"), None, None, None),
            P(("group", "shard"), None, None, None),
            P(None, "shard"),
            P(),
            P("shard", None),
            P("shard", None),
            P(),
        ),
        out_specs=(
            P(("group", "shard"), None, None, None),
            P(("group", "shard"), None, None, None),
            P("group", None, None, None),
        ),
        check_vma=False,
    )
```

```python
import functools

import jax
import jax.numpy as jnp
from jax import lax
from jax.experimental import pallas as pl
from jax.experimental.pallas import tpu as pltpu
from jax.sharding import PartitionSpec as P

BLK = 512
F32, BF16 = jnp.float32, jnp.bfloat16
ROWS, COLS, HALO = 28, 28, 3
PIX = ROWS * COLS
HROWS = ROWS // 2
XROWS, XCOLS = HROWS + 2 * HALO, COLS + 2 * HALO
NT = (((1,), (1,)), ((), ()))
TN = (((0,), (0,)), ((), ()))


def at8(start, size):
    return pl.ds(pl.multiple_of(start, 8), size)


def put_row(x2, half, row, line):
    for blk in range(4):
        start = (row * XCOLS + HALO) * 8 + half * 4 + blk
        x2[pl.ds(start, COLS, stride=8), :] = line[:, 128 * blk : 128 * blk + 128]


def fill_images(x2, img):
    x2[...] = jnp.zeros_like(x2)

    @pl.loop(0, HROWS + HALO)
    def _(i):
        put_row(x2, 0, i + HALO, img[i].astype(F32))
        put_row(x2, 1, i, img[i + HROWS - HALO].astype(F32))


def conv_row(x2, w2, c2, h, flip):
    for w0 in range(0, COLS, 14):
        acc = jnp.zeros((14, 8, 128), F32)
        for a in range(7):
            row = x2[at8(((h + a) * XCOLS + w0) * 8, 160), :].reshape(20, 8, 128)
            for b in range(7):
                tap = 48 - 7 * a - b if flip else 7 * a + b
                acc = acc + row[b : b + 14] * w2[8 * tap : 8 * tap + 8, :][None]
        c2[at8((h * COLS + w0) * 8, 112), :] = acc.reshape(112, 128)


def norm_rows(c2, xhat, rstd, lo, hi):
    @pl.loop(lo, hi)
    def _(k):
        for half in range(2):
            parts = [c2[pl.ds(k * 448 + half * 4 + blk, 56, stride=8), :] for blk in range(4)]
            mean = jnp.sum(parts[0] + parts[1] + parts[2] + parts[3], axis=1, keepdims=True) * (1.0 / 512)
            parts = [v - mean for v in parts]
            sq = [v * v for v in parts]
            var = jnp.sum(sq[0] + sq[1] + sq[2] + sq[3], axis=1, keepdims=True) * (1.0 / 512)
            inv = 1.0 / jnp.sqrt(var + 1e-06)
            rows = at8(half * 392 + k * 56, 56)
            for blk in range(4):
                xhat[rows, 128 * blk : 128 * blk + 128] = parts[blk] * inv
            rstd[rows, :] = jnp.broadcast_to(inv, (56, 128))


def scale_rows(xhat, gain, lhs):
    @pl.loop(0, 7)
    def _(k):
        rows = pl.ds(pl.multiple_of(k * 112, 16), 112)
        lhs[0, rows, :] = (xhat[rows, :] * gain[...]).astype(BF16)


def flat_rows(cot, rhs):
    @pl.loop(0, 7)
    def _(k):
        lines = [cot[4 * k + r].astype(F32) for r in range(4)]
        rhs[4, pl.ds(pl.multiple_of(k * 112, 16), 112), :] = jnp.concatenate(lines, axis=0).astype(BF16)


def gelu_pair(v):
    cdf = 0.5 * (1.0 + lax.erf(v * 0.7071067811865476))
    pdf = 0.3989422804014327 * jnp.exp(-0.5 * v * v)
    return v * cdf, cdf + v * pdf


def up_step(lhs, up, slope, j):
    cols = pl.ds(pl.multiple_of(j * 256, 256), 256)
    part = pl.ds(pl.multiple_of(lax.rem(j, 2) * 256, 256), 256)
    pre = jnp.dot(lhs[0], up[:, cols], preferred_element_type=F32)
    act, der = gelu_pair(pre)
    lhs[1 + lax.div(j, 2), :, part] = act.astype(BF16)
    slope[j] = der


def back_step(rhs, down, slope, j):
    rows = pl.ds(pl.multiple_of(j * 256, 256), 256)
    part = pl.ds(pl.multiple_of(lax.rem(j, 2) * 256, 256), 256)
    back = lax.dot_general(rhs[4], down[rows, :], NT, preferred_element_type=F32)
    rhs[lax.div(j, 2), :, part] = (back * slope[j]).astype(BF16)


def grad_tile(lhs, rhs, k, scale):
    left = jnp.maximum(k - 3, 0)
    right = jnp.minimum(k, 4)
    return lax.dot_general(lhs[left], rhs[right], TN, preferred_element_type=F32) * scale


def branch_cols(lhs, down, out, j):
    cols = pl.ds(pl.multiple_of(j * 256, 256), 256)
    acc = jnp.dot(lhs[1], down[0:512, cols], preferred_element_type=F32)
    for k in range(1, 4):
        acc = acc + jnp.dot(lhs[1 + k], down[512 * k : 512 * k + 512, cols], preferred_element_type=F32)
    out[:, cols] = acc


def back_u_cols(rhs, up, out, j):
    rows = pl.ds(pl.multiple_of(j * 256, 256), 256)
    acc = lax.dot_general(rhs[0], up[rows, 0:512], NT, preferred_element_type=F32)
    for k in range(1, 4):
        acc = acc + lax.dot_general(rhs[k], up[rows, 512 * k : 512 * k + 512], NT, preferred_element_type=F32)
    out[:, rows] = acc


def mix_rows(img, branch, mixed):
    @pl.loop(0, 14)
    def _(k):
        lines = branch[at8(k * 56, 56), :]
        for r in range(2):
            mixed[2 * k + r] = (img[2 * k + r].astype(F32) + lines[28 * r : 28 * r + 28]).astype(BF16)


def norm_back_rows(back, xhat, rstd, gain):
    @pl.loop(0, 14)
    def _(k):
        rows = at8(k * 56, 56)
        grad = back[rows, :] * gain[...]
        unit = xhat[rows, :]
        first = jnp.sum(grad, axis=1, keepdims=True) * (1.0 / 512)
        second = jnp.sum(grad * unit, axis=1, keepdims=True) * (1.0 / 512)
        back[rows, :] = rstd[rows, 0:1] * (grad - first - unit * second)


def fill_back(x2, back):
    @pl.loop(0, 8)
    def _(i):
        lines = back[at8(i * 56, 56), :]
        for r in range(2):
            put_row(x2, 0, 2 * i + r + HALO, lines[28 * r : 28 * r + 28])
        lines = back[at8((i + 6) * 56, 56), :]
        for r in range(2):
            put_row(x2, 1, 2 * i + r + 1, lines[28 * r : 28 * r + 28])

    put_row(x2, 0, 16 + HALO, back[448:476, :])
    put_row(x2, 1, 0, back[308:336, :])


def conv_back_rows(x2, w2, c2, cot, out, lo, hi):
    @pl.loop(lo, hi)
    def _(h):
        conv_row(x2, w2, c2, h, True)
        for half in range(2):
            line = [c2[pl.ds(h * COLS * 8 + half * 4 + blk, COLS, stride=8), :] for blk in range(4)]
            back = jnp.concatenate(line, axis=1)
            out[half * HROWS + h] = (cot[half * HROWS + h].astype(F32) + back).astype(BF16)


MESH = pl.DeviceIdType.MESH
FIRST = 160
PAIRS = [(i, j) for i in range(BLK // 128) for j in range(i, BLK // 128)]


def finish_kernel(mixed_in, out_in, packed_in, mixed, out, stat, lines, packed, blocks, into, back):
    load = pltpu.make_async_copy(packed_in, packed, into.at[8])
    load.start()
    loads, stores = [], []
    for k in range(8):
        rows = pl.ds(7 * (k % 4), 7)
        src, dst = (mixed_in, mixed) if k < 4 else (out_in, out)
        loads.append(pltpu.make_async_copy(src.at[rows], lines.at[k], into.at[k]))
        stores.append(pltpu.make_async_copy(lines.at[k], dst.at[rows], back.at[k]))
    for copy in loads:
        copy.start()
    load.wait()
    for side in range(2):
        for b, (i, j) in enumerate(PAIRS):
            part = packed[side, 128 * b : 128 * b + 128, :].astype(F32)
            blocks[side, 128 * i : 128 * i + 128, 128 * j : 128 * j + 128] = part
            if i != j:
                blocks[side, 128 * j : 128 * j + 128, 128 * i : 128 * i + 128] = part.T
        stores.append(pltpu.make_async_copy(blocks.at[side], stat.at[side], back.at[8 + side]))
        stores[-1].start()
        for k in range(4 * side, 4 * side + 4):
            loads[k].wait()
            stores[k].start()
    for copy in stores:
        copy.wait()


def block_kernel(
    n, img_hbm, cot_hbm, dw, gain, up_in, down_in, owner,
    mixed_hbm, out_hbm, ag,
    x2, w2, c2, xhat, rstd, lhs, rhs, up, down, slope, wide, dwb, flat, p, a0, q, ya, qa, za, zb, qb, yb, gfull, m, c1, img, cot, mixed, out,
    dws, dwr, ups, upr, downs, downr, a0s, a0r, yas, yar, zas, zar, zbs, zbr, ybs, ybr, gs, gr, cs, cr, ds, dr, es, er, ios,
):
    img_copy = pltpu.make_async_copy(img_hbm, img, ios.at[0])
    cot_copy = pltpu.make_async_copy(cot_hbm, cot, ios.at[1])
    mixed_copy = pltpu.make_async_copy(mixed, mixed_hbm, ios.at[2])
    out_copy = pltpu.make_async_copy(out, out_hbm, ios.at[3])
    img_copy.start()
    cot_copy.start()
    g, s = lax.axis_index("group"), lax.axis_index("shard")
    core, pair = lax.rem(s, 2), lax.div(s, 2)
    sib = s + 1 - 2 * core
    tile = BLK
    half, chunk = tile // 2, len(PAIRS) * 128 // n

    def dma(src, dst, ssem, rsem, group, shard):
        return pltpu.make_async_remote_copy(
            src_ref=src, dst_ref=dst, send_sem=ssem, recv_sem=rsem, device_id=(group, shard), device_id_type=MESH
        )

    def peer(i):
        return 2 * lax.rem(pair + i, n) + core

    def gather(mine, place, send, recv):
        def out_copy(i):
            return dma(mine, place(s), send.at[0, i], recv.at[0, i], g, peer(i))

        def on_copy(i):
            j = peer(n - i)
            return dma(mine if i == 0 else place(j), place(s if i == 0 else j), send.at[1, i], recv.at[1, i], g, sib)

        def start():
            on_copy(0).start()
            for i in range(1, n):
                out_copy(i).start()

        def forward():
            for i in range(1, n):
                out_copy(i).wait_recv()
                on_copy(i).start()

        def arrived():
            for i in range(n):
                on_copy(i).wait_recv()

        def finish():
            on_copy(0).wait_send()
            for i in range(1, n):
                out_copy(i).wait_send()
                on_copy(i).wait_send()

        return start, forward, arrived, finish

    zpos, ypos = lax.div(pair, 2), lax.rem(pair, 2)
    across = s + 2 - 4 * ypos
    beyond = g + 1 - 2 * lax.rem(g, 2)

    def spread(place, send, recv):
        def block(i, y):
            return 4 * lax.rem(zpos + 4 - i, 4) + 2 * y + core

        def z_copy(i):
            return dma(place(s), place(s), send.at[0, i], recv.at[0, i], g, 4 * lax.rem(zpos + i, 4) + 2 * ypos + core)

        def y_copy(i, h):
            ref = place(block(i, ypos), h)
            return dma(ref, ref, send.at[1 + h, i], recv.at[1 + h, i], beyond if h else g, across)

        def core_z(i):
            ref = place(block(i, ypos))
            return dma(ref, ref, send.at[3, i], recv.at[3, i], g, sib)

        def core_y(i, h):
            ref = place(block(i, 1 - ypos), h)
            return dma(ref, ref, send.at[4 + h, i], recv.at[4 + h, i], g, sib)

        def start():
            z_copy(1).start()
            z_copy(3).start()
            y_copy(0, 0).start()
            y_copy(0, 1).start()
            core_z(0).start()

        def start_far():
            z_copy(2).start()

        def relay_z(i):
            z_copy(i).wait_recv()
            y_copy(i, 0).start()
            y_copy(i, 1).start()
            core_z(i).start()

        def relay_y(i):
            for h in range(2):
                y_copy(i, h).wait_recv()
                core_y(i, h).start()

        def arrived():
            for i in range(4):
                core_z(i).wait_recv()
                core_y(i, 0).wait_recv()
                core_y(i, 1).wait_recv()

        def finish():
            for i in range(4):
                if i:
                    z_copy(i).wait_send()
                core_z(i).wait_send()
                for h in range(2):
                    y_copy(i, h).wait_send()
                    core_y(i, h).wait_send()

        return start, start_far, relay_z, relay_y, arrived, finish

    mirror = (pair, 2 * g + core)
    barrier = pltpu.get_barrier_semaphore()

    def greet(group, shard):
        pl.semaphore_signal(barrier, inc=1, device_id=(group, shard), device_id_type=MESH)

    for i in range(1, 2 * n):
        greet(g, lax.rem(s + i, 2 * n))
    for i in range(1, n):
        greet(lax.rem(g + i, n), s)

    @pl.when(pair != g)
    def _():
        greet(*mirror)

    greet(beyond, across)

    flat[...] = jnp.zeros_like(flat)
    flat[0:49, :] = dw[...].astype(F32).T
    dwb[s] = jnp.concatenate([flat[16 * t : 16 * t + 16, :] for t in range(4)], axis=1).astype(BF16)
    up[pl.ds(pl.multiple_of(s * 32, 32), 32), :] = up_in[...]
    down[pl.ds(pl.multiple_of(s * 128, 128), 128), :] = down_in[...]
    img_copy.wait()
    fill_images(x2, img)

    def up_place(j, h=None):
        return up.at[pl.ds(pl.multiple_of(j * 32 + (h or 0) * 16, 16), 32 if h is None else 16)]

    def down_place(j, h=None):
        return down.at[pl.ds(pl.multiple_of(j * 128 + (h or 0) * 64, 64), 128 if h is None else 64)]

    up_start, up_far, up_relay_z, up_relay_y, up_arrived, up_finish = spread(up_place, ups, upr)
    down_start, down_far, down_relay_z, down_relay_y, down_arrived, down_finish = spread(down_place, downs, downr)

    def ag_place(j):
        start = lax.div(j, 2) * chunk
        return ag.at[lax.rem(j, 2), pl.ds(pl.multiple_of(start, chunk), chunk)]

    ag_start, ag_forward, ag_arrived, ag_finish = gather(ag_place(s), ag_place, es, er)

    def dw_copy(i):
        return dma(dwb.at[s], dwb.at[s], dws.at[i], dwr.at[i], g, lax.rem(s + i, 2 * n))

    pl.semaphore_wait(barrier, 3 * n - jnp.where(pair == g, 1, 0))
    for i in range(1, 2 * n):
        dw_copy(i).start()
    up_start()
    cot_copy.wait()
    flat_rows(cot, rhs)
    for i in range(1, 2 * n):
        dw_copy(i).wait_recv()
    lane = lax.broadcasted_iota(jnp.int32, (16, 128), 1)
    for blk in range(4):
        lines = [dwb[4 * blk + t].astype(F32) for t in range(4)]
        for k in range(4):
            line = jnp.zeros((16, 128), F32)
            for t in range(4):
                moved = lines[t] if t == k else pltpu.roll(lines[t], 32 * ((t - k) % 4), 1)
                line = jnp.where((lane >= 32 * t) & (lane < 32 * t + 32), moved, line)
            w2[pl.ds(128 * k + blk, 16, stride=8), :] = line
            w2[pl.ds(128 * k + blk + 4, 16, stride=8), :] = line

    def conv_rows(lo, hi):
        @pl.loop(lo, hi)
        def _(h):
            conv_row(x2, w2, c2, h, False)

    up_far()
    conv_rows(0, 3)
    up_relay_z(1)
    up_relay_z(3)
    conv_rows(3, 6)
    down_start()
    conv_rows(6, 9)
    up_relay_z(2)
    conv_rows(9, 12)
    up_relay_y(0)
    up_relay_y(1)
    up_relay_y(3)
    down_far()
    conv_rows(12, HROWS)
    norm_rows(c2, xhat, rstd, 0, 4)
    up_relay_y(2)
    down_relay_z(1)
    down_relay_z(3)
    norm_rows(c2, xhat, rstd, 4, 7)
    scale_rows(xhat, gain, lhs)
    up_arrived()

    def up_steps(lo, hi):
        @pl.loop(lo, hi)
        def _(j):
            up_step(lhs, up, slope, j)

    up_steps(0, 2)
    down_relay_z(2)
    up_steps(2, 6)
    down_relay_y(0)
    down_relay_y(1)
    down_relay_y(3)
    up_steps(6, 8)
    down_relay_y(2)
    down_arrived()

    @pl.loop(0, 8)
    def _(j):
        back_step(rhs, down, slope, j)

    own = pl.ds(pl.multiple_of(core * half, half), half)
    other = pl.ds(pl.multiple_of((1 - core) * half, half), half)
    scale = (2 * n * PIX) ** -0.5

    def slot(i):
        k, same = lax.rem(i, 4), lax.div(i, 4)
        return 2 * lax.rem(zpos + k + 1, 4) + ypos + (1 - same) * (1 - 2 * ypos)

    def along(k):
        return 4 * lax.rem(zpos + k + 1, 4) + 2 * ypos + core

    first, rest = pl.ds(0, FIRST), pl.ds(FIRST, half - FIRST)

    def a0_copy(i):
        return dma(p.at[i, other], a0.at[i], a0s.at[i], a0r.at[i], g, sib)

    def ya_copy(k):
        return dma(q.at[k, first], ya.at[k], yas.at[k], yar.at[k], g, across)

    def za_copy(k):
        return dma(qa.at[k], za.at[k], zas.at[k], zar.at[k], g, along(k))

    def zb_copy(i):
        return dma(q.at[i, rest], zb.at[i], zbs.at[i], zbr.at[i], g, along(lax.rem(i, 4)))

    yb_copy = dma(qb, yb, ybs, ybr, g, across)

    def pass_on(i):
        a0_copy(i).wait_recv()
        q[i] = (p[i, own].astype(F32) + a0[i].astype(F32)).astype(BF16)

        @pl.when(lax.rem(i, 4) < 3)
        def _():
            zb_copy(i).start()

        @pl.when(i < 4)
        def _():
            ya_copy(i).start()

    def turn_first(k):
        ya_copy(k).wait_recv()
        qa[k] = (q[4 + k, first].astype(F32) + ya[k].astype(F32)).astype(BF16)
        za_copy(k).start()

    def rest_sum(base):
        acc = q[base + 3, rest].astype(F32)
        for k in range(3):
            zb_copy(base + k).wait_recv()
            acc = acc + zb[base + k].astype(F32)
        return acc

    @pl.loop(0, n)
    def _(i):
        p[i] = grad_tile(lhs, rhs, owner[slot(i)], scale).astype(BF16)
        a0_copy(i).start()

        @pl.when(i > 0)
        def _():
            pass_on(i - 1)

    @pl.loop(0, 2)
    def _(j):
        branch_cols(lhs, down, wide, j)

    a0_copy(n - 1).wait_recv()
    q[n - 1] = (p[n - 1, own].astype(F32) + a0[n - 1].astype(F32)).astype(BF16)
    mix_rows(img, wide, mixed)
    mixed_copy.start()
    turn_first(0)

    @pl.loop(0, 2)
    def _(j):
        back_u_cols(rhs, up, wide, j)

    turn_first(1)
    norm_back_rows(wide, xhat, rstd, gain)
    fill_back(x2, wide)
    turn_first(2)
    conv_back_rows(x2, w2, c2, cot, out, 0, 4)
    qb[...] = rest_sum(0).astype(BF16)
    yb_copy.start()
    conv_back_rows(x2, w2, c2, cot, out, 4, HROWS)
    out_copy.start()

    acc = rest_sum(4)
    yb_copy.wait_recv()
    gfull[pl.ds(pl.multiple_of(core * half + FIRST, 16), half - FIRST)] = (acc + yb[...].astype(F32)).astype(BF16)
    ya_copy(3).wait_recv()
    acc = q[n - 1, first].astype(F32) + ya[3].astype(F32)
    for k in range(3):
        za_copy(k).wait_recv()
        acc = acc + za[k].astype(F32)
    gfull[pl.ds(pl.multiple_of(core * half, 16), FIRST)] = acc.astype(BF16)
    g_copy = dma(gfull.at[own], gfull.at[own], gs, gr, g, sib)
    g_copy.start()
    g_copy.wait_recv()
    whole = gfull[...]
    side = jnp.where(core == 0, whole, whole.T)
    stat = lax.dot_general(side, side, NT, preferred_element_type=F32)
    stat = (stat * (1.0 / tile)).astype(BF16)
    for b, (i, j) in enumerate(PAIRS):
        m[128 * b : 128 * b + 128, :] = stat[128 * i : 128 * i + 128, 128 * j : 128 * j + 128]

    def m_chunk(j):
        return pl.ds(pl.multiple_of(j * chunk, chunk), chunk)

    def c_copy(i):
        j = lax.rem(g + i, n)
        return dma(m.at[m_chunk(j)], c1.at[i], cs.at[i], cr.at[i], j, s)

    for i in range(1, n):
        c_copy(i).start()
    acc = m[m_chunk(g), :].astype(F32)
    for i in range(1, n):
        c_copy(i).wait_recv()
        acc = acc + c1[i].astype(F32)
    c1[0] = acc.astype(BF16)
    d_copy = dma(c1.at[0], ag_place(mirror[1]), ds, dr, *mirror)

    @pl.when(pair != g)
    def _():
        d_copy.start()
        d_copy.wait_recv()

    @pl.when(pair == g)
    def _():
        ag[core, m_chunk(g), :] = c1[0]

    ag_start()
    ag_forward()
    ag_arrived()
    mixed_copy.wait()
    out_copy.wait()
    up_finish()
    down_finish()
    ag_finish()
    for i in range(1, 2 * n):
        dw_copy(i).wait_send()
    for i in range(n):
        a0_copy(i).wait_send()
    for i in range(n - 1):
        c_copy(i + 1).wait_send()
    for i in range(4):
        ya_copy(i).wait_send()
    for i in range(3):
        za_copy(i).wait_send()
        zb_copy(i).wait_send()
        zb_copy(4 + i).wait_send()
    yb_copy.wait_send()
    g_copy.wait_send()

    @pl.when(pair != g)
    def _():
        d_copy.wait_send()


def local(images, cotangent, dw_kernel, norm_gain, w_up, w_down, owner_table):
    n = lax.axis_size("group")
    half, chunk = BLK // 2, len(PAIRS) * 128 // n
    sem = pltpu.SemaphoreType.DMA
    vmem = pltpu.VMEM
    width = images.shape[-1]
    mixed, back, packed = pl.pallas_call(
        functools.partial(block_kernel, n),
        out_shape=(
            jax.ShapeDtypeStruct((ROWS, COLS, width), BF16),
            jax.ShapeDtypeStruct((ROWS, COLS, width), BF16),
            jax.ShapeDtypeStruct((2, n * chunk, 128), BF16),
        ),
        in_specs=[pl.BlockSpec(memory_space=pl.ANY)] * 2 + [pl.BlockSpec(memory_space=vmem)] * 4 + [pl.BlockSpec(memory_space=pltpu.SMEM)],
        out_specs=[pl.BlockSpec(memory_space=pl.ANY)] * 2 + [pl.BlockSpec(memory_space=vmem)],
        scratch_shapes=[
            vmem((XROWS * XCOLS * 8, 128), F32),
            vmem((512, 128), F32),
            vmem((HROWS * COLS * 8, 128), F32),
            vmem((PIX, width), F32),
            vmem((PIX, 128), F32),
            vmem((5, PIX, width), BF16),
            vmem((5, PIX, width), BF16),
            vmem((512, 2048), BF16),
            vmem((2048, 512), BF16),
            vmem((8, PIX, 256), F32),
            vmem((PIX, width), F32),
            vmem((2 * n, 16, 128), BF16),
            vmem((64, 32), F32),
            vmem((n, BLK, BLK), BF16),
            vmem((n, half, BLK), BF16),
            vmem((n, half, BLK), BF16),
            vmem((4, FIRST, BLK), BF16),
            vmem((3, FIRST, BLK), BF16),
            vmem((3, FIRST, BLK), BF16),
            vmem((7, half - FIRST, BLK), BF16),
            vmem((half - FIRST, BLK), BF16),
            vmem((half - FIRST, BLK), BF16),
            vmem((BLK, BLK), BF16),
            vmem((n * chunk, 128), BF16),
            vmem((n, chunk, 128), BF16),
            vmem((ROWS, COLS, width), BF16),
            vmem((ROWS, COLS, width), BF16),
            vmem((ROWS, COLS, width), BF16),
            vmem((ROWS, COLS, width), BF16),
            sem((2 * n,)), sem((2 * n,)),
            sem((6, 4)), sem((6, 4)),
            sem((6, 4)), sem((6, 4)),
            sem((n,)), sem((n,)),
            sem((4,)), sem((4,)),
            sem((3,)), sem((3,)),
            sem((7,)), sem((7,)),
            sem, sem,
            sem, sem,
            sem((n,)), sem((n,)),
            sem, sem,
            sem((2, n)), sem((2, n)),
            sem((4,)),
        ],
        compiler_params=pltpu.CompilerParams(collective_id=0, has_side_effects=True, vmem_limit_bytes=60 * 2**20),
    )(images[0], cotangent[0], dw_kernel.T, norm_gain.reshape(1, width), w_up, w_down, owner_table)
    mixed, back, stat = pl.pallas_call(
        finish_kernel,
        out_shape=(
            jax.ShapeDtypeStruct((ROWS, COLS, width), BF16),
            jax.ShapeDtypeStruct((ROWS, COLS, width), BF16),
            jax.ShapeDtypeStruct((2, BLK, BLK), F32),
        ),
        in_specs=[pl.BlockSpec(memory_space=pl.ANY)] * 3,
        out_specs=[pl.BlockSpec(memory_space=pl.ANY)] * 3,
        scratch_shapes=[
            vmem((8, 7, COLS, width), BF16),
            vmem((2, n * chunk, 128), BF16),
            vmem((2, BLK, BLK), F32),
            sem((9,)), sem((10,)),
        ],
        compiler_params=pltpu.CompilerParams(vmem_limit_bytes=60 * 2**20),
    )(mixed, back, packed)
    return (mixed[None], back[None], stat[None])


def solution(mesh):
    return jax.shard_map(
        local,
        mesh=mesh,
        in_specs=(
            P(("group", "shard"), None, None, None),
            P(("group", "shard"), None, None, None),
            P(None, "shard"),
            P(),
            P("shard", None),
            P("shard", None),
            P(),
        ),
        out_specs=(
            P(("group", "shard"), None, None, None),
            P(("group", "shard"), None, None, None),
            P("group", None, None, None),
        ),
        check_vma=False,
    )
```

```python
import functools

import jax
import jax.numpy as jnp
from jax import lax
from jax.experimental import pallas as pl
from jax.experimental.pallas import tpu as pltpu
from jax.sharding import PartitionSpec as P

BLK = 512
F32, BF16 = jnp.float32, jnp.bfloat16
ROWS, COLS, HALO = 28, 28, 3
PIX = ROWS * COLS
HROWS = ROWS // 2
XROWS, XCOLS = HROWS + 2 * HALO, COLS + 2 * HALO
NT = (((1,), (1,)), ((), ()))
TN = (((0,), (0,)), ((), ()))


def at8(start, size):
    return pl.ds(pl.multiple_of(start, 8), size)


def put_row(x2, half, row, line):
    for blk in range(4):
        start = (row * XCOLS + HALO) * 8 + half * 4 + blk
        x2[pl.ds(start, COLS, stride=8), :] = line[:, 128 * blk : 128 * blk + 128]


def fill_images(x2, img):
    x2[...] = jnp.zeros_like(x2)

    @pl.loop(0, HROWS + HALO)
    def _(i):
        put_row(x2, 0, i + HALO, img[i].astype(F32))
        put_row(x2, 1, i, img[i + HROWS - HALO].astype(F32))


def conv_row(x2, w2, c2, h, flip):
    for w0 in range(0, COLS, 14):
        acc = jnp.zeros((14, 8, 128), F32)
        for a in range(7):
            row = x2[at8(((h + a) * XCOLS + w0) * 8, 160), :].reshape(20, 8, 128)
            for b in range(7):
                tap = 48 - 7 * a - b if flip else 7 * a + b
                acc = acc + row[b : b + 14] * w2[8 * tap : 8 * tap + 8, :][None]
        c2[at8((h * COLS + w0) * 8, 112), :] = acc.reshape(112, 128)


def norm_rows(c2, xhat, rstd, lo, hi):
    @pl.loop(lo, hi)
    def _(k):
        for half in range(2):
            parts = [c2[pl.ds(k * 448 + half * 4 + blk, 56, stride=8), :] for blk in range(4)]
            mean = jnp.sum(parts[0] + parts[1] + parts[2] + parts[3], axis=1, keepdims=True) * (1.0 / 512)
            parts = [v - mean for v in parts]
            sq = [v * v for v in parts]
            var = jnp.sum(sq[0] + sq[1] + sq[2] + sq[3], axis=1, keepdims=True) * (1.0 / 512)
            inv = 1.0 / jnp.sqrt(var + 1e-06)
            rows = at8(half * 392 + k * 56, 56)
            for blk in range(4):
                xhat[rows, 128 * blk : 128 * blk + 128] = parts[blk] * inv
            rstd[rows, :] = jnp.broadcast_to(inv, (56, 128))


def scale_rows(xhat, gain, lhs):
    @pl.loop(0, 7)
    def _(k):
        rows = pl.ds(pl.multiple_of(k * 112, 16), 112)
        lhs[0, rows, :] = (xhat[rows, :] * gain[...]).astype(BF16)


def flat_rows(cot, rhs):
    @pl.loop(0, 7)
    def _(k):
        lines = [cot[4 * k + r].astype(F32) for r in range(4)]
        rhs[4, pl.ds(pl.multiple_of(k * 112, 16), 112), :] = jnp.concatenate(lines, axis=0).astype(BF16)


def gelu_pair(v):
    cdf = 0.5 * (1.0 + lax.erf(v * 0.7071067811865476))
    pdf = 0.3989422804014327 * jnp.exp(-0.5 * v * v)
    return v * cdf, cdf + v * pdf


def up_step(lhs, up, slope, j):
    cols = pl.ds(pl.multiple_of(j * 256, 256), 256)
    part = pl.ds(pl.multiple_of(lax.rem(j, 2) * 256, 256), 256)
    pre = jnp.dot(lhs[0], up[:, cols], preferred_element_type=F32)
    act, der = gelu_pair(pre)
    lhs[1 + lax.div(j, 2), :, part] = act.astype(BF16)
    slope[j] = der


def back_step(rhs, down, slope, j):
    rows = pl.ds(pl.multiple_of(j * 256, 256), 256)
    part = pl.ds(pl.multiple_of(lax.rem(j, 2) * 256, 256), 256)
    back = lax.dot_general(rhs[4], down[rows, :], NT, preferred_element_type=F32)
    rhs[lax.div(j, 2), :, part] = (back * slope[j]).astype(BF16)


def grad_tile(lhs, rhs, k, scale):
    left = jnp.maximum(k - 3, 0)
    right = jnp.minimum(k, 4)
    return lax.dot_general(lhs[left], rhs[right], TN, preferred_element_type=F32) * scale


def branch_cols(lhs, down, out, j):
    cols = pl.ds(pl.multiple_of(j * 256, 256), 256)
    acc = jnp.dot(lhs[1], down[0:512, cols], preferred_element_type=F32)
    for k in range(1, 4):
        acc = acc + jnp.dot(lhs[1 + k], down[512 * k : 512 * k + 512, cols], preferred_element_type=F32)
    out[:, cols] = acc


def back_u_cols(rhs, up, out, j):
    rows = pl.ds(pl.multiple_of(j * 256, 256), 256)
    acc = lax.dot_general(rhs[0], up[rows, 0:512], NT, preferred_element_type=F32)
    for k in range(1, 4):
        acc = acc + lax.dot_general(rhs[k], up[rows, 512 * k : 512 * k + 512], NT, preferred_element_type=F32)
    out[:, rows] = acc


def mix_rows(img, branch, mixed):
    @pl.loop(0, 14)
    def _(k):
        lines = branch[at8(k * 56, 56), :]
        for r in range(2):
            mixed[2 * k + r] = (img[2 * k + r].astype(F32) + lines[28 * r : 28 * r + 28]).astype(BF16)


def norm_back_rows(back, xhat, rstd, gain):
    @pl.loop(0, 14)
    def _(k):
        rows = at8(k * 56, 56)
        grad = back[rows, :] * gain[...]
        unit = xhat[rows, :]
        first = jnp.sum(grad, axis=1, keepdims=True) * (1.0 / 512)
        second = jnp.sum(grad * unit, axis=1, keepdims=True) * (1.0 / 512)
        back[rows, :] = rstd[rows, 0:1] * (grad - first - unit * second)


def fill_back(x2, back):
    @pl.loop(0, 8)
    def _(i):
        lines = back[at8(i * 56, 56), :]
        for r in range(2):
            put_row(x2, 0, 2 * i + r + HALO, lines[28 * r : 28 * r + 28])
        lines = back[at8((i + 6) * 56, 56), :]
        for r in range(2):
            put_row(x2, 1, 2 * i + r + 1, lines[28 * r : 28 * r + 28])

    put_row(x2, 0, 16 + HALO, back[448:476, :])
    put_row(x2, 1, 0, back[308:336, :])


def conv_back_rows(x2, w2, c2, cot, out, lo, hi):
    @pl.loop(lo, hi)
    def _(h):
        conv_row(x2, w2, c2, h, True)
        for half in range(2):
            line = [c2[pl.ds(h * COLS * 8 + half * 4 + blk, COLS, stride=8), :] for blk in range(4)]
            back = jnp.concatenate(line, axis=1)
            out[half * HROWS + h] = (cot[half * HROWS + h].astype(F32) + back).astype(BF16)


MESH = pl.DeviceIdType.MESH
FIRST = 160
PAIRS = [(i, j) for i in range(BLK // 128) for j in range(i, BLK // 128)]


def finish_kernel(mixed_in, out_in, packed_in, mixed, out, stat, lines, packed, blocks, into, back):
    load = pltpu.make_async_copy(packed_in, packed, into.at[8])
    load.start()
    loads, stores = [], []
    for k in range(8):
        rows = pl.ds(7 * (k % 4), 7)
        src, dst = (mixed_in, mixed) if k < 4 else (out_in, out)
        loads.append(pltpu.make_async_copy(src.at[rows], lines.at[k], into.at[k]))
        stores.append(pltpu.make_async_copy(lines.at[k], dst.at[rows], back.at[k]))
    for copy in loads:
        copy.start()
    load.wait()
    for side in range(2):
        for b, (i, j) in enumerate(PAIRS):
            part = packed[side, 128 * b : 128 * b + 128, :].astype(F32)
            blocks[side, 128 * i : 128 * i + 128, 128 * j : 128 * j + 128] = part
            if i != j:
                blocks[side, 128 * j : 128 * j + 128, 128 * i : 128 * i + 128] = part.T
        stores.append(pltpu.make_async_copy(blocks.at[side], stat.at[side], back.at[8 + side]))
        stores[-1].start()
        for k in range(4 * side, 4 * side + 4):
            loads[k].wait()
            stores[k].start()
    for copy in stores:
        copy.wait()


def block_kernel(
    n, img_hbm, cot_hbm, dw_hbm, gain_hbm, up_hbm, down_hbm, owner,
    mixed_hbm, out_hbm, ag,
    x2, w2, c2, xhat, rstd, lhs, rhs, up, down, slope, wide, dwb, flat, p, a0, q, ya, qa, za, zb, qb, yb, gfull, m, c1, img, cot, mixed, out, dw, gain,
    dws, dwr, ups, upr, downs, downr, a0s, a0r, yas, yar, zas, zar, zbs, zbr, ybs, ybr, gs, gr, cs, cr, ds, dr, es, er, ios,
):
    img_copy = pltpu.make_async_copy(img_hbm, img, ios.at[0])
    cot_copy = pltpu.make_async_copy(cot_hbm, cot, ios.at[1])
    mixed_copy = pltpu.make_async_copy(mixed, mixed_hbm, ios.at[2])
    out_copy = pltpu.make_async_copy(out, out_hbm, ios.at[3])
    g, s = lax.axis_index("group"), lax.axis_index("shard")
    core, pair = lax.rem(s, 2), lax.div(s, 2)
    sib = s + 1 - 2 * core
    tile = BLK
    half, chunk = tile // 2, len(PAIRS) * 128 // n

    def dma(src, dst, ssem, rsem, group, shard):
        return pltpu.make_async_remote_copy(
            src_ref=src, dst_ref=dst, send_sem=ssem, recv_sem=rsem, device_id=(group, shard), device_id_type=MESH
        )

    def peer(i):
        return 2 * lax.rem(pair + i, n) + core

    def gather(mine, place, send, recv, base):
        def out_copy(i):
            return dma(mine, place(s), send.at[base, i], recv.at[base, i], g, peer(i))

        def on_copy(i):
            j = peer(n - i)
            return dma(mine if i == 0 else place(j), place(s if i == 0 else j), send.at[base + 1, i], recv.at[base + 1, i], g, sib)

        def start():
            on_copy(0).start()
            for i in range(1, n):
                out_copy(i).start()

        def forward():
            for i in range(1, n):
                out_copy(i).wait_recv()
                on_copy(i).start()

        def arrived():
            for i in range(n):
                on_copy(i).wait_recv()

        def finish():
            on_copy(0).wait_send()
            for i in range(1, n):
                out_copy(i).wait_send()
                on_copy(i).wait_send()

        return start, forward, arrived, finish

    zpos, ypos = lax.div(pair, 2), lax.rem(pair, 2)
    across = s + 2 - 4 * ypos
    beyond = g + 1 - 2 * lax.rem(g, 2)

    def spread(place, send, recv):
        def block(i, y):
            return 4 * lax.rem(zpos + 4 - i, 4) + 2 * y + core

        def z_copy(i):
            return dma(place(s), place(s), send.at[0, i], recv.at[0, i], g, 4 * lax.rem(zpos + i, 4) + 2 * ypos + core)

        def y_copy(i, h):
            ref = place(block(i, ypos), h)
            return dma(ref, ref, send.at[1 + h, i], recv.at[1 + h, i], beyond if h else g, across)

        def core_z(i):
            ref = place(block(i, ypos))
            return dma(ref, ref, send.at[3, i], recv.at[3, i], g, sib)

        def core_y(i, h):
            ref = place(block(i, 1 - ypos), h)
            return dma(ref, ref, send.at[4 + h, i], recv.at[4 + h, i], g, sib)

        def start():
            z_copy(1).start()
            z_copy(3).start()
            y_copy(0, 0).start()
            y_copy(0, 1).start()
            core_z(0).start()

        def start_far():
            z_copy(2).start()

        def relay_z(i):
            z_copy(i).wait_recv()
            y_copy(i, 0).start()
            y_copy(i, 1).start()
            core_z(i).start()

        def relay_y(i):
            for h in range(2):
                y_copy(i, h).wait_recv()
                core_y(i, h).start()

        def arrived():
            for i in range(4):
                core_z(i).wait_recv()
                core_y(i, 0).wait_recv()
                core_y(i, 1).wait_recv()

        def finish():
            for i in range(4):
                if i:
                    z_copy(i).wait_send()
                core_z(i).wait_send()
                for h in range(2):
                    y_copy(i, h).wait_send()
                    core_y(i, h).wait_send()

        return start, start_far, relay_z, relay_y, arrived, finish

    mirror = (pair, 2 * g + core)
    barrier = pltpu.get_barrier_semaphore()

    def greet(group, shard):
        pl.semaphore_signal(barrier, inc=1, device_id=(group, shard), device_id_type=MESH)

    for i in range(1, 2 * n):
        greet(g, lax.rem(s + i, 2 * n))
    for i in range(1, n):
        greet(lax.rem(g + i, n), s)

    @pl.when(pair != g)
    def _():
        greet(*mirror)

    greet(beyond, across)

    small = [
        pltpu.make_async_copy(dw_hbm, dw, ios.at[4]),
        pltpu.make_async_copy(up_hbm, up.at[pl.ds(pl.multiple_of(s * 32, 32), 32)], ios.at[5]),
        pltpu.make_async_copy(down_hbm, down.at[pl.ds(pl.multiple_of(s * 128, 128), 128)], ios.at[6]),
        pltpu.make_async_copy(gain_hbm, gain, ios.at[7]),
    ]
    for copy in small[:2]:
        copy.start()
    img_copy.start()
    cot_copy.start()
    for copy in small[2:]:
        copy.start()
    small[0].wait()

    flat[...] = jnp.zeros_like(flat)
    flat[0:49, :] = dw[...].astype(F32).T
    dwb[s] = jnp.concatenate([flat[16 * t : 16 * t + 16, :] for t in range(4)], axis=1).astype(BF16)
    img_copy.wait()
    fill_images(x2, img)
    for copy in small[1:]:
        copy.wait()

    def up_place(j, h=None):
        return up.at[pl.ds(pl.multiple_of(j * 32 + (h or 0) * 16, 16), 32 if h is None else 16)]

    def down_place(j, h=None):
        return down.at[pl.ds(pl.multiple_of(j * 128 + (h or 0) * 64, 64), 128 if h is None else 64)]

    up_start, up_far, up_relay_z, up_relay_y, up_arrived, up_finish = spread(up_place, ups, upr)
    down_start, down_far, down_relay_z, down_relay_y, down_arrived, down_finish = spread(down_place, downs, downr)

    part = chunk // 2

    def ag_place(j, h):
        return ag.at[lax.rem(j, 2), pl.ds(pl.multiple_of(lax.div(j, 2) * chunk + h * part, part), part)]

    gathers = [gather(ag_place(s, h), lambda j, h=h: ag_place(j, h), es, er, 2 * h) for h in range(2)]

    def dw_copy(i):
        return dma(dwb.at[s], dwb.at[s], dws.at[i], dwr.at[i], g, lax.rem(s + i, 2 * n))

    pl.semaphore_wait(barrier, 3 * n - jnp.where(pair == g, 1, 0))
    for i in range(1, 2 * n):
        dw_copy(i).start()
    up_start()
    up_far()
    down_start()
    cot_copy.wait()
    flat_rows(cot, rhs)
    for i in range(1, 2 * n):
        dw_copy(i).wait_recv()
    lane = lax.broadcasted_iota(jnp.int32, (16, 128), 1)
    for blk in range(4):
        lines = [dwb[4 * blk + t].astype(F32) for t in range(4)]
        for k in range(4):
            line = jnp.zeros((16, 128), F32)
            for t in range(4):
                moved = lines[t] if t == k else pltpu.roll(lines[t], 32 * ((t - k) % 4), 1)
                line = jnp.where((lane >= 32 * t) & (lane < 32 * t + 32), moved, line)
            w2[pl.ds(128 * k + blk, 16, stride=8), :] = line
            w2[pl.ds(128 * k + blk + 4, 16, stride=8), :] = line

    def conv_rows(lo, hi):
        @pl.loop(lo, hi)
        def _(h):
            conv_row(x2, w2, c2, h, False)

    conv_rows(0, 4)
    up_relay_z(1)
    up_relay_z(3)
    up_relay_z(2)
    down_far()
    conv_rows(4, 12)
    up_relay_y(0)
    up_relay_y(1)
    up_relay_y(3)
    conv_rows(12, HROWS)
    down_relay_z(1)
    down_relay_z(3)
    norm_rows(c2, xhat, rstd, 0, 4)
    up_relay_y(2)
    norm_rows(c2, xhat, rstd, 4, 7)
    scale_rows(xhat, gain, lhs)
    down_relay_z(2)
    up_arrived()

    def up_steps(lo, hi):
        @pl.loop(lo, hi)
        def _(j):
            up_step(lhs, up, slope, j)

    up_steps(0, 4)
    down_relay_y(0)
    down_relay_y(1)
    down_relay_y(3)
    up_steps(4, 7)
    down_relay_y(2)
    up_steps(7, 8)
    down_arrived()

    @pl.loop(0, 8)
    def _(j):
        back_step(rhs, down, slope, j)

    own = pl.ds(pl.multiple_of(core * half, half), half)
    other = pl.ds(pl.multiple_of((1 - core) * half, half), half)
    scale = (2 * n * PIX) ** -0.5

    def slot(i):
        k, same = lax.rem(i, 4), lax.div(i, 4)
        return 2 * lax.rem(zpos + k + 1, 4) + ypos + (1 - same) * (1 - 2 * ypos)

    def along(k):
        return 4 * lax.rem(zpos + k + 1, 4) + 2 * ypos + core

    first, rest = pl.ds(0, FIRST), pl.ds(FIRST, half - FIRST)

    def a0_copy(i):
        return dma(p.at[i, other], a0.at[i], a0s.at[i], a0r.at[i], g, sib)

    def ya_copy(k):
        return dma(q.at[k, first], ya.at[k], yas.at[k], yar.at[k], g, across)

    def za_copy(k):
        return dma(qa.at[k], za.at[k], zas.at[k], zar.at[k], g, along(k))

    def zb_copy(i):
        return dma(q.at[i, rest], zb.at[i], zbs.at[i], zbr.at[i], g, along(lax.rem(i, 4)))

    yb_copy = dma(qb, yb, ybs, ybr, g, across)

    def pass_on(i):
        a0_copy(i).wait_recv()
        q[i] = (p[i, own].astype(F32) + a0[i].astype(F32)).astype(BF16)

        @pl.when(lax.rem(i, 4) < 3)
        def _():
            zb_copy(i).start()

        @pl.when(i < 4)
        def _():
            ya_copy(i).start()

    def turn_first(k):
        ya_copy(k).wait_recv()
        qa[k] = (q[4 + k, first].astype(F32) + ya[k].astype(F32)).astype(BF16)
        za_copy(k).start()

    def rest_sum(base):
        acc = q[base + 3, rest].astype(F32)
        for k in range(3):
            zb_copy(base + k).wait_recv()
            acc = acc + zb[base + k].astype(F32)
        return acc

    @pl.loop(0, n)
    def _(i):
        p[i] = grad_tile(lhs, rhs, owner[slot(i)], scale).astype(BF16)
        a0_copy(i).start()

        @pl.when(i > 0)
        def _():
            pass_on(i - 1)

    @pl.loop(0, 2)
    def _(j):
        branch_cols(lhs, down, wide, j)

    a0_copy(n - 1).wait_recv()
    q[n - 1] = (p[n - 1, own].astype(F32) + a0[n - 1].astype(F32)).astype(BF16)
    mix_rows(img, wide, mixed)
    mixed_copy.start()
    turn_first(0)

    @pl.loop(0, 2)
    def _(j):
        back_u_cols(rhs, up, wide, j)

    turn_first(1)
    norm_back_rows(wide, xhat, rstd, gain)
    fill_back(x2, wide)
    turn_first(2)
    conv_back_rows(x2, w2, c2, cot, out, 0, 3)
    qb[...] = rest_sum(0).astype(BF16)
    yb_copy.start()
    conv_back_rows(x2, w2, c2, cot, out, 3, 5)

    acc = rest_sum(4)
    yb_copy.wait_recv()
    gfull[pl.ds(pl.multiple_of(core * half + FIRST, 16), half - FIRST)] = (acc + yb[...].astype(F32)).astype(BF16)
    ya_copy(3).wait_recv()
    acc = q[n - 1, first].astype(F32) + ya[3].astype(F32)
    for k in range(3):
        za_copy(k).wait_recv()
        acc = acc + za[k].astype(F32)
    gfull[pl.ds(pl.multiple_of(core * half, 16), FIRST)] = acc.astype(BF16)
    g_copy = dma(gfull.at[own], gfull.at[own], gs, gr, g, sib)
    g_copy.start()
    g_copy.wait_recv()
    whole = gfull[...]
    side = jnp.where(core == 0, whole, whole.T)
    stat = lax.dot_general(side, side, NT, preferred_element_type=F32)
    stat = (stat * (1.0 / tile)).astype(BF16)
    for b, (i, j) in enumerate(PAIRS):
        m[128 * b : 128 * b + 128, :] = stat[128 * i : 128 * i + 128, 128 * j : 128 * j + 128]

    def m_part(j, h):
        return pl.ds(pl.multiple_of(j * chunk + h * part, part), part)

    def c_copy(i, h):
        j = lax.rem(g + i, n)
        return dma(m.at[m_part(j, h)], c1.at[i, pl.ds(h * part, part)], cs.at[h, i], cr.at[h, i], j, s)

    def d_copy(h):
        return dma(c1.at[0, pl.ds(h * part, part)], ag_place(mirror[1], h), ds.at[h], dr.at[h], *mirror)

    for h in range(2):
        for i in range(1, n):
            c_copy(i, h).start()
    conv_back_rows(x2, w2, c2, cot, out, 5, 9)
    for h in range(2):
        acc = m[m_part(g, h), :].astype(F32)
        for i in range(1, n):
            c_copy(i, h).wait_recv()
            acc = acc + c1[i, part * h : part * h + part, :].astype(F32)
        total = acc.astype(BF16)
        c1[0, part * h : part * h + part, :] = total

        @pl.when(pair != g)
        def _():
            d_copy(h).start()

        @pl.when(pair == g)
        def _():
            ag[core, m_part(g, h), :] = total

    conv_back_rows(x2, w2, c2, cot, out, 9, 11)
    for h in range(2):

        @pl.when(pair != g)
        def _():
            d_copy(h).wait_recv()

        gathers[h][0]()

    conv_back_rows(x2, w2, c2, cot, out, 11, HROWS)
    out_copy.start()
    for h in range(2):
        gathers[h][1]()
    for h in range(2):
        gathers[h][2]()

    mixed_copy.wait()
    out_copy.wait()
    up_finish()
    down_finish()
    for h in range(2):
        gathers[h][3]()
    for i in range(1, 2 * n):
        dw_copy(i).wait_send()
    for i in range(n):
        a0_copy(i).wait_send()
    for i in range(n - 1):
        c_copy(i + 1, 0).wait_send()
        c_copy(i + 1, 1).wait_send()
    for i in range(4):
        ya_copy(i).wait_send()
    for i in range(3):
        za_copy(i).wait_send()
        zb_copy(i).wait_send()
        zb_copy(4 + i).wait_send()
    yb_copy.wait_send()
    g_copy.wait_send()

    @pl.when(pair != g)
    def _():
        d_copy(0).wait_send()
        d_copy(1).wait_send()


def local(images, cotangent, dw_kernel, norm_gain, w_up, w_down, owner_table):
    n = lax.axis_size("group")
    half, chunk = BLK // 2, len(PAIRS) * 128 // n
    sem = pltpu.SemaphoreType.DMA
    vmem = pltpu.VMEM
    width = images.shape[-1]
    mixed, back, packed = pl.pallas_call(
        functools.partial(block_kernel, n),
        out_shape=(
            jax.ShapeDtypeStruct((ROWS, COLS, width), BF16),
            jax.ShapeDtypeStruct((ROWS, COLS, width), BF16),
            jax.ShapeDtypeStruct((2, n * chunk, 128), BF16),
        ),
        in_specs=[pl.BlockSpec(memory_space=pl.ANY)] * 6 + [pl.BlockSpec(memory_space=pltpu.SMEM)],
        out_specs=[pl.BlockSpec(memory_space=pl.ANY)] * 2 + [pl.BlockSpec(memory_space=vmem)],
        scratch_shapes=[
            vmem((XROWS * XCOLS * 8, 128), F32),
            vmem((512, 128), F32),
            vmem((HROWS * COLS * 8, 128), F32),
            vmem((PIX, width), F32),
            vmem((PIX, 128), F32),
            vmem((5, PIX, width), BF16),
            vmem((5, PIX, width), BF16),
            vmem((512, 2048), BF16),
            vmem((2048, 512), BF16),
            vmem((8, PIX, 256), F32),
            vmem((PIX, width), F32),
            vmem((2 * n, 16, 128), BF16),
            vmem((64, 32), F32),
            vmem((n, BLK, BLK), BF16),
            vmem((n, half, BLK), BF16),
            vmem((n, half, BLK), BF16),
            vmem((4, FIRST, BLK), BF16),
            vmem((3, FIRST, BLK), BF16),
            vmem((3, FIRST, BLK), BF16),
            vmem((7, half - FIRST, BLK), BF16),
            vmem((half - FIRST, BLK), BF16),
            vmem((half - FIRST, BLK), BF16),
            vmem((BLK, BLK), BF16),
            vmem((n * chunk, 128), BF16),
            vmem((n, chunk, 128), BF16),
            vmem((ROWS, COLS, width), BF16),
            vmem((ROWS, COLS, width), BF16),
            vmem((ROWS, COLS, width), BF16),
            vmem((ROWS, COLS, width), BF16),
            vmem((32, 49), BF16),
            vmem((1, width), F32),
            sem((2 * n,)), sem((2 * n,)),
            sem((6, 4)), sem((6, 4)),
            sem((6, 4)), sem((6, 4)),
            sem((n,)), sem((n,)),
            sem((4,)), sem((4,)),
            sem((3,)), sem((3,)),
            sem((7,)), sem((7,)),
            sem, sem,
            sem, sem,
            sem((2, n)), sem((2, n)),
            sem((2,)), sem((2,)),
            sem((4, n)), sem((4, n)),
            sem((8,)),
        ],
        compiler_params=pltpu.CompilerParams(collective_id=0, has_side_effects=True, vmem_limit_bytes=60 * 2**20),
    )(images[0], cotangent[0], dw_kernel.T, norm_gain.reshape(1, width), w_up, w_down, owner_table)
    mixed, back, stat = pl.pallas_call(
        finish_kernel,
        out_shape=(
            jax.ShapeDtypeStruct((ROWS, COLS, width), BF16),
            jax.ShapeDtypeStruct((ROWS, COLS, width), BF16),
            jax.ShapeDtypeStruct((2, BLK, BLK), F32),
        ),
        in_specs=[pl.BlockSpec(memory_space=pl.ANY)] * 3,
        out_specs=[pl.BlockSpec(memory_space=pl.ANY)] * 3,
        scratch_shapes=[
            vmem((8, 7, COLS, width), BF16),
            vmem((2, n * chunk, 128), BF16),
            vmem((2, BLK, BLK), F32),
            sem((9,)), sem((10,)),
        ],
        compiler_params=pltpu.CompilerParams(vmem_limit_bytes=60 * 2**20),
    )(mixed, back, packed)
    return (mixed[None], back[None], stat[None])


def solution(mesh):
    return jax.shard_map(
        local,
        mesh=mesh,
        in_specs=(
            P(("group", "shard"), None, None, None),
            P(("group", "shard"), None, None, None),
            P(None, "shard"),
            P(),
            P("shard", None),
            P("shard", None),
            P(),
        ),
        out_specs=(
            P(("group", "shard"), None, None, None),
            P(("group", "shard"), None, None, None),
            P("group", None, None, None),
        ),
        check_vma=False,
    )
```

```python
import functools

import jax
import jax.numpy as jnp
from jax import lax
from jax.experimental import pallas as pl
from jax.experimental.pallas import tpu as pltpu
from jax.sharding import PartitionSpec as P

BLK = 512
F32, BF16 = jnp.float32, jnp.bfloat16
ROWS, COLS, HALO = 28, 28, 3
PIX = ROWS * COLS
HROWS = ROWS // 2
XROWS, XCOLS = HROWS + 2 * HALO, COLS + 2 * HALO
NT = (((1,), (1,)), ((), ()))
TN = (((0,), (0,)), ((), ()))


def at8(start, size):
    return pl.ds(pl.multiple_of(start, 8), size)


def put_row(x2, half, row, line):
    for blk in range(4):
        start = (row * XCOLS + HALO) * 8 + half * 4 + blk
        x2[pl.ds(start, COLS, stride=8), :] = line[:, 128 * blk : 128 * blk + 128]


def fill_images(x2, img):
    x2[...] = jnp.zeros_like(x2)

    @pl.loop(0, HROWS + HALO)
    def _(i):
        put_row(x2, 0, i + HALO, img[i].astype(F32))
        put_row(x2, 1, i, img[i + HROWS - HALO].astype(F32))


def conv_row(x2, w2, c2, h, flip):
    for w0 in range(0, COLS, 14):
        acc = jnp.zeros((14, 8, 128), F32)
        for a in range(7):
            row = x2[at8(((h + a) * XCOLS + w0) * 8, 160), :].reshape(20, 8, 128)
            for b in range(7):
                tap = 48 - 7 * a - b if flip else 7 * a + b
                acc = acc + row[b : b + 14] * w2[8 * tap : 8 * tap + 8, :][None]
        c2[at8((h * COLS + w0) * 8, 112), :] = acc.reshape(112, 128)


def norm_rows(c2, xhat, rstd, lo, hi):
    @pl.loop(lo, hi)
    def _(k):
        for half in range(2):
            parts = [c2[pl.ds(k * 448 + half * 4 + blk, 56, stride=8), :] for blk in range(4)]
            mean = jnp.sum(parts[0] + parts[1] + parts[2] + parts[3], axis=1, keepdims=True) * (1.0 / 512)
            parts = [v - mean for v in parts]
            sq = [v * v for v in parts]
            var = jnp.sum(sq[0] + sq[1] + sq[2] + sq[3], axis=1, keepdims=True) * (1.0 / 512)
            inv = 1.0 / jnp.sqrt(var + 1e-06)
            rows = at8(half * 392 + k * 56, 56)
            for blk in range(4):
                xhat[rows, 128 * blk : 128 * blk + 128] = parts[blk] * inv
            rstd[rows, :] = jnp.broadcast_to(inv, (56, 128))


def scale_rows(xhat, gain, lhs):
    @pl.loop(0, 7)
    def _(k):
        rows = pl.ds(pl.multiple_of(k * 112, 16), 112)
        lhs[0, rows, :] = (xhat[rows, :] * gain[...]).astype(BF16)


def flat_rows(cot, rhs):
    @pl.loop(0, 7)
    def _(k):
        lines = [cot[4 * k + r].astype(F32) for r in range(4)]
        rhs[4, pl.ds(pl.multiple_of(k * 112, 16), 112), :] = jnp.concatenate(lines, axis=0).astype(BF16)


def gelu_pair(v):
    cdf = 0.5 * (1.0 + lax.erf(v * 0.7071067811865476))
    pdf = 0.3989422804014327 * jnp.exp(-0.5 * v * v)
    return v * cdf, cdf + v * pdf


def up_step(lhs, up, slope, j):
    cols = pl.ds(pl.multiple_of(j * 256, 256), 256)
    part = pl.ds(pl.multiple_of(lax.rem(j, 2) * 256, 256), 256)
    pre = jnp.dot(lhs[0], up[:, cols], preferred_element_type=F32)
    act, der = gelu_pair(pre)
    lhs[1 + lax.div(j, 2), :, part] = act.astype(BF16)
    slope[j] = der


def back_step(rhs, down, slope, j):
    rows = pl.ds(pl.multiple_of(j * 256, 256), 256)
    part = pl.ds(pl.multiple_of(lax.rem(j, 2) * 256, 256), 256)
    back = lax.dot_general(rhs[4], down[rows, :], NT, preferred_element_type=F32)
    rhs[lax.div(j, 2), :, part] = (back * slope[j]).astype(BF16)


def grad_tile(lhs, rhs, k, scale):
    left = jnp.maximum(k - 3, 0)
    right = jnp.minimum(k, 4)
    return lax.dot_general(lhs[left], rhs[right], TN, preferred_element_type=F32) * scale


def branch_cols(lhs, down, out, j):
    cols = pl.ds(pl.multiple_of(j * 256, 256), 256)
    acc = jnp.dot(lhs[1], down[0:512, cols], preferred_element_type=F32)
    for k in range(1, 4):
        acc = acc + jnp.dot(lhs[1 + k], down[512 * k : 512 * k + 512, cols], preferred_element_type=F32)
    out[:, cols] = acc


def back_u_cols(rhs, up, out, j):
    rows = pl.ds(pl.multiple_of(j * 256, 256), 256)
    acc = lax.dot_general(rhs[0], up[rows, 0:512], NT, preferred_element_type=F32)
    for k in range(1, 4):
        acc = acc + lax.dot_general(rhs[k], up[rows, 512 * k : 512 * k + 512], NT, preferred_element_type=F32)
    out[:, rows] = acc


def mix_rows(img, branch, mixed):
    @pl.loop(0, 14)
    def _(k):
        lines = branch[at8(k * 56, 56), :]
        for r in range(2):
            mixed[2 * k + r] = (img[2 * k + r].astype(F32) + lines[28 * r : 28 * r + 28]).astype(BF16)


def norm_back_rows(back, xhat, rstd, gain):
    @pl.loop(0, 14)
    def _(k):
        rows = at8(k * 56, 56)
        grad = back[rows, :] * gain[...]
        unit = xhat[rows, :]
        first = jnp.sum(grad, axis=1, keepdims=True) * (1.0 / 512)
        second = jnp.sum(grad * unit, axis=1, keepdims=True) * (1.0 / 512)
        back[rows, :] = rstd[rows, 0:1] * (grad - first - unit * second)


def fill_back(x2, back):
    @pl.loop(0, 8)
    def _(i):
        lines = back[at8(i * 56, 56), :]
        for r in range(2):
            put_row(x2, 0, 2 * i + r + HALO, lines[28 * r : 28 * r + 28])
        lines = back[at8((i + 6) * 56, 56), :]
        for r in range(2):
            put_row(x2, 1, 2 * i + r + 1, lines[28 * r : 28 * r + 28])

    put_row(x2, 0, 16 + HALO, back[448:476, :])
    put_row(x2, 1, 0, back[308:336, :])


def conv_back_rows(x2, w2, c2, cot, out, lo, hi):
    @pl.loop(lo, hi)
    def _(h):
        conv_row(x2, w2, c2, h, True)
        for half in range(2):
            line = [c2[pl.ds(h * COLS * 8 + half * 4 + blk, COLS, stride=8), :] for blk in range(4)]
            back = jnp.concatenate(line, axis=1)
            out[half * HROWS + h] = (cot[half * HROWS + h].astype(F32) + back).astype(BF16)


MESH = pl.DeviceIdType.MESH
FIRST = 144
PAIRS = [(i, j) for i in range(BLK // 128) for j in range(i, BLK // 128)]


def finish_kernel(mixed_in, out_in, packed_in, mixed, out, stat, lines, packed, blocks, into, back):
    load = pltpu.make_async_copy(packed_in, packed, into.at[8])
    load.start()
    loads, stores = [], []
    for k in range(8):
        rows = pl.ds(7 * (k % 4), 7)
        src, dst = (mixed_in, mixed) if k < 4 else (out_in, out)
        loads.append(pltpu.make_async_copy(src.at[rows], lines.at[k], into.at[k]))
        stores.append(pltpu.make_async_copy(lines.at[k], dst.at[rows], back.at[k]))
    for copy in loads:
        copy.start()
    load.wait()
    for side in range(2):
        for b, (i, j) in enumerate(PAIRS):
            part = packed[side, 128 * b : 128 * b + 128, :].astype(F32)
            blocks[side, 128 * i : 128 * i + 128, 128 * j : 128 * j + 128] = part
            if i != j:
                blocks[side, 128 * j : 128 * j + 128, 128 * i : 128 * i + 128] = part.T
        stores.append(pltpu.make_async_copy(blocks.at[side], stat.at[side], back.at[8 + side]))
        stores[-1].start()
        for k in range(4 * side, 4 * side + 4):
            loads[k].wait()
            stores[k].start()
    for copy in stores:
        copy.wait()


def block_kernel(
    n, img_hbm, cot_hbm, dw_hbm, gain_hbm, up_hbm, down_hbm, owner,
    mixed_hbm, out_hbm, ag,
    x2, w2, c2, xhat, rstd, lhs, rhs, up, down, slope, wide, dwb, flat, p, a0, q, ya, qa, za, zb, qb, yb, gfull, m, c1, img, cot, mixed, out, dw, gain,
    dws, dwr, ups, upr, downs, downr, a0s, a0r, yas, yar, zas, zar, zbs, zbr, ybs, ybr, gs, gr, cs, cr, ds, dr, es, er, ios,
):
    img_copy = pltpu.make_async_copy(img_hbm, img, ios.at[0])
    cot_copy = pltpu.make_async_copy(cot_hbm, cot, ios.at[1])
    mixed_copy = pltpu.make_async_copy(mixed, mixed_hbm, ios.at[2])
    out_copy = pltpu.make_async_copy(out, out_hbm, ios.at[3])
    g, s = lax.axis_index("group"), lax.axis_index("shard")
    core, pair = lax.rem(s, 2), lax.div(s, 2)
    sib = s + 1 - 2 * core
    tile = BLK
    half, chunk = tile // 2, len(PAIRS) * 128 // n

    def dma(src, dst, ssem, rsem, group, shard):
        return pltpu.make_async_remote_copy(
            src_ref=src, dst_ref=dst, send_sem=ssem, recv_sem=rsem, device_id=(group, shard), device_id_type=MESH
        )

    def peer(i):
        return 2 * lax.rem(pair + i, n) + core

    def gather(mine, place, send, recv, base):
        def out_copy(i):
            return dma(mine, place(s), send.at[base, i], recv.at[base, i], g, peer(i))

        def on_copy(i):
            j = peer(n - i)
            return dma(mine if i == 0 else place(j), place(s if i == 0 else j), send.at[base + 1, i], recv.at[base + 1, i], g, sib)

        def start():
            on_copy(0).start()
            for i in range(1, n):
                out_copy(i).start()

        def forward():
            for i in range(1, n):
                out_copy(i).wait_recv()
                on_copy(i).start()

        def arrived():
            for i in range(n):
                on_copy(i).wait_recv()

        def finish():
            on_copy(0).wait_send()
            for i in range(1, n):
                out_copy(i).wait_send()
                on_copy(i).wait_send()

        return start, forward, arrived, finish

    zpos, ypos = lax.div(pair, 2), lax.rem(pair, 2)
    across = s + 2 - 4 * ypos
    beyond = g + 1 - 2 * lax.rem(g, 2)

    def spread(place, send, recv):
        def block(i, y):
            return 4 * lax.rem(zpos + 4 - i, 4) + 2 * y + core

        def z_copy(i):
            return dma(place(s), place(s), send.at[0, i], recv.at[0, i], g, 4 * lax.rem(zpos + i, 4) + 2 * ypos + core)

        def y_copy(i, h):
            ref = place(block(i, ypos), h)
            return dma(ref, ref, send.at[1 + h, i], recv.at[1 + h, i], beyond if h else g, across)

        def core_z(i):
            ref = place(block(i, ypos))
            return dma(ref, ref, send.at[3, i], recv.at[3, i], g, sib)

        def core_y(i, h):
            ref = place(block(i, 1 - ypos), h)
            return dma(ref, ref, send.at[4 + h, i], recv.at[4 + h, i], g, sib)

        def start():
            z_copy(1).start()
            z_copy(3).start()
            y_copy(0, 0).start()
            y_copy(0, 1).start()
            core_z(0).start()

        def start_far():
            z_copy(2).start()

        def relay_z(i):
            z_copy(i).wait_recv()
            y_copy(i, 0).start()
            y_copy(i, 1).start()
            core_z(i).start()

        def relay_y(i):
            for h in range(2):
                y_copy(i, h).wait_recv()
                core_y(i, h).start()

        def arrived():
            for i in range(4):
                core_z(i).wait_recv()
                core_y(i, 0).wait_recv()
                core_y(i, 1).wait_recv()

        def finish():
            for i in range(4):
                if i:
                    z_copy(i).wait_send()
                core_z(i).wait_send()
                for h in range(2):
                    y_copy(i, h).wait_send()
                    core_y(i, h).wait_send()

        return start, start_far, relay_z, relay_y, arrived, finish

    mirror = (pair, 2 * g + core)
    barrier = pltpu.get_barrier_semaphore()

    def greet(group, shard):
        pl.semaphore_signal(barrier, inc=1, device_id=(group, shard), device_id_type=MESH)

    for i in range(1, 2 * n):
        greet(g, lax.rem(s + i, 2 * n))
    for i in range(1, n):
        greet(lax.rem(g + i, n), s)

    @pl.when(pair != g)
    def _():
        greet(*mirror)

    greet(beyond, across)

    small = [
        pltpu.make_async_copy(dw_hbm, dw, ios.at[4]),
        pltpu.make_async_copy(up_hbm, up.at[pl.ds(pl.multiple_of(s * 32, 32), 32)], ios.at[5]),
        pltpu.make_async_copy(down_hbm, down.at[pl.ds(pl.multiple_of(s * 128, 128), 128)], ios.at[6]),
        pltpu.make_async_copy(gain_hbm, gain, ios.at[7]),
    ]
    for copy in small[:2]:
        copy.start()
    img_copy.start()
    cot_copy.start()
    for copy in small[2:]:
        copy.start()
    small[0].wait()

    flat[...] = jnp.zeros_like(flat)
    flat[0:49, :] = dw[...].astype(F32).T
    dwb[s] = jnp.concatenate([flat[16 * t : 16 * t + 16, :] for t in range(4)], axis=1).astype(BF16)
    img_copy.wait()
    fill_images(x2, img)
    for copy in small[1:]:
        copy.wait()

    def up_place(j, h=None):
        return up.at[pl.ds(pl.multiple_of(j * 32 + (h or 0) * 16, 16), 32 if h is None else 16)]

    def down_place(j, h=None):
        return down.at[pl.ds(pl.multiple_of(j * 128 + (h or 0) * 64, 64), 128 if h is None else 64)]

    up_start, up_far, up_relay_z, up_relay_y, up_arrived, up_finish = spread(up_place, ups, upr)
    down_start, down_far, down_relay_z, down_relay_y, down_arrived, down_finish = spread(down_place, downs, downr)

    part = chunk // 2

    def ag_place(j, h):
        return ag.at[lax.rem(j, 2), pl.ds(pl.multiple_of(lax.div(j, 2) * chunk + h * part, part), part)]

    gathers = [gather(ag_place(s, h), lambda j, h=h: ag_place(j, h), es, er, 2 * h) for h in range(2)]

    def dw_copy(i):
        return dma(dwb.at[s], dwb.at[s], dws.at[i], dwr.at[i], g, lax.rem(s + i, 2 * n))

    pl.semaphore_wait(barrier, 3 * n - jnp.where(pair == g, 1, 0))
    for i in range(1, 2 * n):
        dw_copy(i).start()
    up_start()
    up_far()
    down_start()
    cot_copy.wait()
    flat_rows(cot, rhs)
    for i in range(1, 2 * n):
        dw_copy(i).wait_recv()
    lane = lax.broadcasted_iota(jnp.int32, (16, 128), 1)
    for blk in range(4):
        lines = [dwb[4 * blk + t].astype(F32) for t in range(4)]
        for k in range(4):
            line = jnp.zeros((16, 128), F32)
            for t in range(4):
                moved = lines[t] if t == k else pltpu.roll(lines[t], 32 * ((t - k) % 4), 1)
                line = jnp.where((lane >= 32 * t) & (lane < 32 * t + 32), moved, line)
            w2[pl.ds(128 * k + blk, 16, stride=8), :] = line
            w2[pl.ds(128 * k + blk + 4, 16, stride=8), :] = line

    def conv_rows(lo, hi):
        @pl.loop(lo, hi)
        def _(h):
            conv_row(x2, w2, c2, h, False)

    conv_rows(0, 4)
    up_relay_z(1)
    up_relay_z(3)
    up_relay_z(2)
    down_far()
    conv_rows(4, 12)
    up_relay_y(0)
    up_relay_y(1)
    up_relay_y(3)
    conv_rows(12, HROWS)
    down_relay_z(1)
    down_relay_z(3)
    norm_rows(c2, xhat, rstd, 0, 4)
    up_relay_y(2)
    norm_rows(c2, xhat, rstd, 4, 7)
    scale_rows(xhat, gain, lhs)
    down_relay_z(2)
    up_arrived()

    def up_steps(lo, hi):
        @pl.loop(lo, hi)
        def _(j):
            up_step(lhs, up, slope, j)

    up_steps(0, 4)
    down_relay_y(0)
    down_relay_y(1)
    down_relay_y(3)
    up_steps(4, 7)
    down_relay_y(2)
    up_steps(7, 8)
    down_arrived()

    @pl.loop(0, 8)
    def _(j):
        back_step(rhs, down, slope, j)

    own = pl.ds(pl.multiple_of(core * half, half), half)
    other = pl.ds(pl.multiple_of((1 - core) * half, half), half)
    scale = (2 * n * PIX) ** -0.5

    def slot(i):
        k, same = lax.rem(i, 4), lax.div(i, 4)
        return 2 * lax.rem(zpos + k + 1, 4) + ypos + (1 - same) * (1 - 2 * ypos)

    def along(k):
        return 4 * lax.rem(zpos + k + 1, 4) + 2 * ypos + core

    first, rest = pl.ds(0, FIRST), pl.ds(FIRST, half - FIRST)

    def a0_copy(i):
        return dma(p.at[i, other], a0.at[i], a0s.at[i], a0r.at[i], g, sib)

    def ya_copy(k):
        return dma(q.at[k, first], ya.at[k], yas.at[k], yar.at[k], g, across)

    def za_copy(k):
        return dma(qa.at[k], za.at[k], zas.at[k], zar.at[k], g, along(k))

    def zb_copy(i):
        return dma(q.at[i, rest], zb.at[i], zbs.at[i], zbr.at[i], g, along(lax.rem(i, 4)))

    yb_copy = dma(qb, yb, ybs, ybr, g, across)

    def pass_on(i):
        a0_copy(i).wait_recv()
        q[i] = (p[i, own].astype(F32) + a0[i].astype(F32)).astype(BF16)

        @pl.when(lax.rem(i, 4) < 3)
        def _():
            zb_copy(i).start()

        @pl.when(i < 4)
        def _():
            ya_copy(i).start()

    def turn_first(k):
        ya_copy(k).wait_recv()
        qa[k] = (q[4 + k, first].astype(F32) + ya[k].astype(F32)).astype(BF16)
        za_copy(k).start()

    def rest_sum(base):
        acc = q[base + 3, rest].astype(F32)
        for k in range(3):
            zb_copy(base + k).wait_recv()
            acc = acc + zb[base + k].astype(F32)
        return acc

    @pl.loop(0, n)
    def _(i):
        p[i] = grad_tile(lhs, rhs, owner[slot(i)], scale).astype(BF16)
        a0_copy(i).start()

        @pl.when(i > 0)
        def _():
            pass_on(i - 1)

    @pl.loop(0, 2)
    def _(j):
        branch_cols(lhs, down, wide, j)

    a0_copy(n - 1).wait_recv()
    q[n - 1] = (p[n - 1, own].astype(F32) + a0[n - 1].astype(F32)).astype(BF16)
    mix_rows(img, wide, mixed)
    mixed_copy.start()
    turn_first(0)

    @pl.loop(0, 2)
    def _(j):
        back_u_cols(rhs, up, wide, j)

    turn_first(1)
    norm_back_rows(wide, xhat, rstd, gain)
    fill_back(x2, wide)
    turn_first(2)
    conv_back_rows(x2, w2, c2, cot, out, 0, 3)
    qb[...] = rest_sum(0).astype(BF16)
    yb_copy.start()
    conv_back_rows(x2, w2, c2, cot, out, 3, 5)

    acc = rest_sum(4)
    yb_copy.wait_recv()
    gfull[pl.ds(pl.multiple_of(core * half + FIRST, 16), half - FIRST)] = (acc + yb[...].astype(F32)).astype(BF16)
    ya_copy(3).wait_recv()
    acc = q[n - 1, first].astype(F32) + ya[3].astype(F32)
    for k in range(3):
        za_copy(k).wait_recv()
        acc = acc + za[k].astype(F32)
    gfull[pl.ds(pl.multiple_of(core * half, 16), FIRST)] = acc.astype(BF16)
    g_copy = dma(gfull.at[own], gfull.at[own], gs, gr, g, sib)
    g_copy.start()
    g_copy.wait_recv()
    whole = gfull[...]
    side = jnp.where(core == 0, whole, whole.T)
    stat = lax.dot_general(side, side, NT, preferred_element_type=F32)
    stat = (stat * (1.0 / tile)).astype(BF16)
    for b, (i, j) in enumerate(PAIRS):
        m[128 * b : 128 * b + 128, :] = stat[128 * i : 128 * i + 128, 128 * j : 128 * j + 128]

    def m_part(j, h):
        return pl.ds(pl.multiple_of(j * chunk + h * part, part), part)

    def c_copy(i, h):
        j = lax.rem(g + i, n)
        return dma(m.at[m_part(j, h)], c1.at[i, pl.ds(h * part, part)], cs.at[h, i], cr.at[h, i], j, s)

    def d_copy(h):
        return dma(c1.at[0, pl.ds(h * part, part)], ag_place(mirror[1], h), ds.at[h], dr.at[h], *mirror)

    for h in range(2):
        for i in range(1, n):
            c_copy(i, h).start()
    conv_back_rows(x2, w2, c2, cot, out, 5, 9)
    for h in range(2):
        acc = m[m_part(g, h), :].astype(F32)
        for i in range(1, n):
            c_copy(i, h).wait_recv()
            acc = acc + c1[i, part * h : part * h + part, :].astype(F32)
        total = acc.astype(BF16)
        c1[0, part * h : part * h + part, :] = total

        @pl.when(pair != g)
        def _():
            d_copy(h).start()

        @pl.when(pair == g)
        def _():
            ag[core, m_part(g, h), :] = total

    conv_back_rows(x2, w2, c2, cot, out, 9, 11)
    for h in range(2):

        @pl.when(pair != g)
        def _():
            d_copy(h).wait_recv()

        gathers[h][0]()

    conv_back_rows(x2, w2, c2, cot, out, 11, HROWS)
    out_copy.start()
    for h in range(2):
        gathers[h][1]()
    for h in range(2):
        gathers[h][2]()

    mixed_copy.wait()
    out_copy.wait()
    up_finish()
    down_finish()
    for h in range(2):
        gathers[h][3]()
    for i in range(1, 2 * n):
        dw_copy(i).wait_send()
    for i in range(n):
        a0_copy(i).wait_send()
    for i in range(n - 1):
        c_copy(i + 1, 0).wait_send()
        c_copy(i + 1, 1).wait_send()
    for i in range(4):
        ya_copy(i).wait_send()
    for i in range(3):
        za_copy(i).wait_send()
        zb_copy(i).wait_send()
        zb_copy(4 + i).wait_send()
    yb_copy.wait_send()
    g_copy.wait_send()

    @pl.when(pair != g)
    def _():
        d_copy(0).wait_send()
        d_copy(1).wait_send()


def local(images, cotangent, dw_kernel, norm_gain, w_up, w_down, owner_table):
    n = lax.axis_size("group")
    half, chunk = BLK // 2, len(PAIRS) * 128 // n
    sem = pltpu.SemaphoreType.DMA
    vmem = pltpu.VMEM
    width = images.shape[-1]
    mixed, back, packed = pl.pallas_call(
        functools.partial(block_kernel, n),
        out_shape=(
            jax.ShapeDtypeStruct((ROWS, COLS, width), BF16),
            jax.ShapeDtypeStruct((ROWS, COLS, width), BF16),
            jax.ShapeDtypeStruct((2, n * chunk, 128), BF16),
        ),
        in_specs=[pl.BlockSpec(memory_space=pl.ANY)] * 6 + [pl.BlockSpec(memory_space=pltpu.SMEM)],
        out_specs=[pl.BlockSpec(memory_space=pl.ANY)] * 2 + [pl.BlockSpec(memory_space=vmem)],
        scratch_shapes=[
            vmem((XROWS * XCOLS * 8, 128), F32),
            vmem((512, 128), F32),
            vmem((HROWS * COLS * 8, 128), F32),
            vmem((PIX, width), F32),
            vmem((PIX, 128), F32),
            vmem((5, PIX, width), BF16),
            vmem((5, PIX, width), BF16),
            vmem((512, 2048), BF16),
            vmem((2048, 512), BF16),
            vmem((8, PIX, 256), F32),
            vmem((PIX, width), F32),
            vmem((2 * n, 16, 128), BF16),
            vmem((64, 32), F32),
            vmem((n, BLK, BLK), BF16),
            vmem((n, half, BLK), BF16),
            vmem((n, half, BLK), BF16),
            vmem((4, FIRST, BLK), BF16),
            vmem((3, FIRST, BLK), BF16),
            vmem((3, FIRST, BLK), BF16),
            vmem((7, half - FIRST, BLK), BF16),
            vmem((half - FIRST, BLK), BF16),
            vmem((half - FIRST, BLK), BF16),
            vmem((BLK, BLK), BF16),
            vmem((n * chunk, 128), BF16),
            vmem((n, chunk, 128), BF16),
            vmem((ROWS, COLS, width), BF16),
            vmem((ROWS, COLS, width), BF16),
            vmem((ROWS, COLS, width), BF16),
            vmem((ROWS, COLS, width), BF16),
            vmem((32, 49), BF16),
            vmem((1, width), F32),
            sem((2 * n,)), sem((2 * n,)),
            sem((6, 4)), sem((6, 4)),
            sem((6, 4)), sem((6, 4)),
            sem((n,)), sem((n,)),
            sem((4,)), sem((4,)),
            sem((3,)), sem((3,)),
            sem((7,)), sem((7,)),
            sem, sem,
            sem, sem,
            sem((2, n)), sem((2, n)),
            sem((2,)), sem((2,)),
            sem((4, n)), sem((4, n)),
            sem((8,)),
        ],
        compiler_params=pltpu.CompilerParams(collective_id=0, has_side_effects=True, vmem_limit_bytes=60 * 2**20),
    )(images[0], cotangent[0], dw_kernel.T, norm_gain.reshape(1, width), w_up, w_down, owner_table)
    mixed, back, stat = pl.pallas_call(
        finish_kernel,
        out_shape=(
            jax.ShapeDtypeStruct((ROWS, COLS, width), BF16),
            jax.ShapeDtypeStruct((ROWS, COLS, width), BF16),
            jax.ShapeDtypeStruct((2, BLK, BLK), F32),
        ),
        in_specs=[pl.BlockSpec(memory_space=pl.ANY)] * 3,
        out_specs=[pl.BlockSpec(memory_space=pl.ANY)] * 3,
        scratch_shapes=[
            vmem((8, 7, COLS, width), BF16),
            vmem((2, n * chunk, 128), BF16),
            vmem((2, BLK, BLK), F32),
            sem((9,)), sem((10,)),
        ],
        compiler_params=pltpu.CompilerParams(vmem_limit_bytes=60 * 2**20),
    )(mixed, back, packed)
    return (mixed[None], back[None], stat[None])


def solution(mesh):
    return jax.shard_map(
        local,
        mesh=mesh,
        in_specs=(
            P(("group", "shard"), None, None, None),
            P(("group", "shard"), None, None, None),
            P(None, "shard"),
            P(),
            P("shard", None),
            P("shard", None),
            P(),
        ),
        out_specs=(
            P(("group", "shard"), None, None, None),
            P(("group", "shard"), None, None, None),
            P("group", None, None, None),
        ),
        check_vma=False,
    )
```

```python
import functools

import jax
import jax.numpy as jnp
from jax import lax
from jax.experimental import pallas as pl
from jax.experimental.pallas import tpu as pltpu
from jax.sharding import PartitionSpec as P

BLK = 512
F32, BF16 = jnp.float32, jnp.bfloat16
ROWS, COLS, HALO = 28, 28, 3
PIX = ROWS * COLS
HROWS = ROWS // 2
XROWS, XCOLS = HROWS + 2 * HALO, COLS + 2 * HALO
NT = (((1,), (1,)), ((), ()))
TN = (((0,), (0,)), ((), ()))


def at8(start, size):
    return pl.ds(pl.multiple_of(start, 8), size)


def put_row(x2, half, row, line):
    for blk in range(4):
        start = (row * XCOLS + HALO) * 8 + half * 4 + blk
        x2[pl.ds(start, COLS, stride=8), :] = line[:, 128 * blk : 128 * blk + 128]


def fill_images(x2, img):
    x2[...] = jnp.zeros_like(x2)

    @pl.loop(0, HROWS + HALO)
    def _(i):
        put_row(x2, 0, i + HALO, img[i].astype(F32))
        put_row(x2, 1, i, img[i + HROWS - HALO].astype(F32))


def conv_row(x2, w2, c2, h, flip):
    for w0 in range(0, COLS, 14):
        acc = jnp.zeros((14, 8, 128), F32)
        for a in range(7):
            row = x2[at8(((h + a) * XCOLS + w0) * 8, 160), :].reshape(20, 8, 128)
            for b in range(7):
                tap = 48 - 7 * a - b if flip else 7 * a + b
                acc = acc + row[b : b + 14] * w2[8 * tap : 8 * tap + 8, :][None]
        c2[at8((h * COLS + w0) * 8, 112), :] = acc.reshape(112, 128)


def norm_rows(c2, xhat, rstd, lo, hi):
    @pl.loop(lo, hi)
    def _(k):
        for half in range(2):
            parts = [c2[pl.ds(k * 448 + half * 4 + blk, 56, stride=8), :] for blk in range(4)]
            mean = jnp.sum(parts[0] + parts[1] + parts[2] + parts[3], axis=1, keepdims=True) * (1.0 / 512)
            parts = [v - mean for v in parts]
            sq = [v * v for v in parts]
            var = jnp.sum(sq[0] + sq[1] + sq[2] + sq[3], axis=1, keepdims=True) * (1.0 / 512)
            inv = 1.0 / jnp.sqrt(var + 1e-06)
            rows = at8(half * 392 + k * 56, 56)
            for blk in range(4):
                xhat[rows, 128 * blk : 128 * blk + 128] = parts[blk] * inv
            rstd[rows, :] = jnp.broadcast_to(inv, (56, 128))


def scale_rows(xhat, gain, lhs):
    @pl.loop(0, 7)
    def _(k):
        rows = pl.ds(pl.multiple_of(k * 112, 16), 112)
        lhs[0, rows, :] = (xhat[rows, :] * gain[...]).astype(BF16)


def flat_rows(cot, rhs):
    @pl.loop(0, 7)
    def _(k):
        lines = [cot[4 * k + r].astype(F32) for r in range(4)]
        rhs[4, pl.ds(pl.multiple_of(k * 112, 16), 112), :] = jnp.concatenate(lines, axis=0).astype(BF16)


def gelu_pair(v):
    cdf = 0.5 * (1.0 + lax.erf(v * 0.7071067811865476))
    pdf = 0.3989422804014327 * jnp.exp(-0.5 * v * v)
    return v * cdf, cdf + v * pdf


def up_step(lhs, up, slope, j):
    cols = pl.ds(pl.multiple_of(j * 256, 256), 256)
    part = pl.ds(pl.multiple_of(lax.rem(j, 2) * 256, 256), 256)
    pre = jnp.dot(lhs[0], up[:, cols], preferred_element_type=F32)
    act, der = gelu_pair(pre)
    lhs[1 + lax.div(j, 2), :, part] = act.astype(BF16)
    slope[j] = der


def back_step(rhs, down, slope, j):
    rows = pl.ds(pl.multiple_of(j * 256, 256), 256)
    part = pl.ds(pl.multiple_of(lax.rem(j, 2) * 256, 256), 256)
    back = lax.dot_general(rhs[4], down[rows, :], NT, preferred_element_type=F32)
    rhs[lax.div(j, 2), :, part] = (back * slope[j]).astype(BF16)


def grad_tile(lhs, rhs, k, scale):
    left = jnp.maximum(k - 3, 0)
    right = jnp.minimum(k, 4)
    return lax.dot_general(lhs[left], rhs[right], TN, preferred_element_type=F32) * scale


def branch_cols(lhs, down, out, j):
    cols = pl.ds(pl.multiple_of(j * 256, 256), 256)
    acc = jnp.dot(lhs[1], down[0:512, cols], preferred_element_type=F32)
    for k in range(1, 4):
        acc = acc + jnp.dot(lhs[1 + k], down[512 * k : 512 * k + 512, cols], preferred_element_type=F32)
    out[:, cols] = acc


def back_u_cols(rhs, up, out, j):
    rows = pl.ds(pl.multiple_of(j * 256, 256), 256)
    acc = lax.dot_general(rhs[0], up[rows, 0:512], NT, preferred_element_type=F32)
    for k in range(1, 4):
        acc = acc + lax.dot_general(rhs[k], up[rows, 512 * k : 512 * k + 512], NT, preferred_element_type=F32)
    out[:, rows] = acc


def mix_rows(img, branch, mixed):
    @pl.loop(0, 14)
    def _(k):
        lines = branch[at8(k * 56, 56), :]
        for r in range(2):
            mixed[2 * k + r] = (img[2 * k + r].astype(F32) + lines[28 * r : 28 * r + 28]).astype(BF16)


def norm_back_rows(back, xhat, rstd, gain):
    @pl.loop(0, 14)
    def _(k):
        rows = at8(k * 56, 56)
        grad = back[rows, :] * gain[...]
        unit = xhat[rows, :]
        first = jnp.sum(grad, axis=1, keepdims=True) * (1.0 / 512)
        second = jnp.sum(grad * unit, axis=1, keepdims=True) * (1.0 / 512)
        back[rows, :] = rstd[rows, 0:1] * (grad - first - unit * second)


def fill_back(x2, back):
    @pl.loop(0, 8)
    def _(i):
        lines = back[at8(i * 56, 56), :]
        for r in range(2):
            put_row(x2, 0, 2 * i + r + HALO, lines[28 * r : 28 * r + 28])
        lines = back[at8((i + 6) * 56, 56), :]
        for r in range(2):
            put_row(x2, 1, 2 * i + r + 1, lines[28 * r : 28 * r + 28])

    put_row(x2, 0, 16 + HALO, back[448:476, :])
    put_row(x2, 1, 0, back[308:336, :])


def conv_back_rows(x2, w2, c2, cot, out, lo, hi):
    @pl.loop(lo, hi)
    def _(h):
        conv_row(x2, w2, c2, h, True)
        for half in range(2):
            line = [c2[pl.ds(h * COLS * 8 + half * 4 + blk, COLS, stride=8), :] for blk in range(4)]
            back = jnp.concatenate(line, axis=1)
            out[half * HROWS + h] = (cot[half * HROWS + h].astype(F32) + back).astype(BF16)


MESH = pl.DeviceIdType.MESH
FIRST = 144
PAIRS = [(i, j) for i in range(BLK // 128) for j in range(i, BLK // 128)]


def finish_kernel(mixed_in, out_in, packed_in, mixed, out, stat, lines, packed, blocks, into, back):
    load = pltpu.make_async_copy(packed_in, packed, into.at[8])
    load.start()
    loads, stores = [], []
    for k in range(8):
        rows = pl.ds(7 * (k % 4), 7)
        src, dst = (mixed_in, mixed) if k < 4 else (out_in, out)
        loads.append(pltpu.make_async_copy(src.at[rows], lines.at[k], into.at[k]))
        stores.append(pltpu.make_async_copy(lines.at[k], dst.at[rows], back.at[k]))
    for copy in loads:
        copy.start()
    for k in range(8):
        loads[k].wait()
        stores[k].start()
    load.wait()
    for side in range(2):
        for b, (i, j) in enumerate(PAIRS):
            part = packed[side, 128 * b : 128 * b + 128, :].astype(F32)
            blocks[side, 128 * i : 128 * i + 128, 128 * j : 128 * j + 128] = part
            if i != j:
                blocks[side, 128 * j : 128 * j + 128, 128 * i : 128 * i + 128] = part.T
        stores.append(pltpu.make_async_copy(blocks.at[side], stat.at[side], back.at[8 + side]))
        stores[-1].start()
    for copy in stores:
        copy.wait()


def block_kernel(
    n, img_hbm, cot_hbm, dw_hbm, gain_hbm, up_hbm, down_hbm, owner,
    mixed_hbm, out_hbm, ag,
    x2, w2, c2, xhat, rstd, lhs, rhs, up, down, slope, wide, dwb, flat, p, a0, q, ya, qa, za, zb, qb, yb, gfull, m, c1, img, cot, mixed, out, dw, gain,
    dws, dwr, ups, upr, downs, downr, a0s, a0r, yas, yar, zas, zar, zbs, zbr, ybs, ybr, gs, gr, cs, cr, ds, dr, es, er, ios,
):
    img_copy = pltpu.make_async_copy(img_hbm, img, ios.at[0])
    cot_copy = pltpu.make_async_copy(cot_hbm, cot, ios.at[1])
    mixed_copy = pltpu.make_async_copy(mixed, mixed_hbm, ios.at[2])
    out_copy = pltpu.make_async_copy(out, out_hbm, ios.at[3])
    g, s = lax.axis_index("group"), lax.axis_index("shard")
    core, pair = lax.rem(s, 2), lax.div(s, 2)
    sib = s + 1 - 2 * core
    tile = BLK
    half, chunk = tile // 2, len(PAIRS) * 128 // n

    def dma(src, dst, ssem, rsem, group, shard):
        return pltpu.make_async_remote_copy(
            src_ref=src, dst_ref=dst, send_sem=ssem, recv_sem=rsem, device_id=(group, shard), device_id_type=MESH
        )

    def peer(i):
        return 2 * lax.rem(pair + i, n) + core

    def gather(mine, place, send, recv, base):
        def out_copy(i):
            return dma(mine, place(s), send.at[base, i], recv.at[base, i], g, peer(i))

        def on_copy(i):
            j = peer(n - i)
            return dma(mine if i == 0 else place(j), place(s if i == 0 else j), send.at[base + 1, i], recv.at[base + 1, i], g, sib)

        def start():
            on_copy(0).start()
            for i in range(1, n):
                out_copy(i).start()

        def forward():
            for i in range(1, n):
                out_copy(i).wait_recv()
                on_copy(i).start()

        def arrived():
            for i in range(n):
                on_copy(i).wait_recv()

        def finish():
            on_copy(0).wait_send()
            for i in range(1, n):
                out_copy(i).wait_send()
                on_copy(i).wait_send()

        return start, forward, arrived, finish

    zpos, ypos = lax.div(pair, 2), lax.rem(pair, 2)
    across = s + 2 - 4 * ypos
    beyond = g + 1 - 2 * lax.rem(g, 2)

    def spread(place, send, recv):
        def block(i, y):
            return 4 * lax.rem(zpos + 4 - i, 4) + 2 * y + core

        def z_copy(i):
            return dma(place(s), place(s), send.at[0, i], recv.at[0, i], g, 4 * lax.rem(zpos + i, 4) + 2 * ypos + core)

        def y_copy(i, h):
            ref = place(block(i, ypos), h)
            return dma(ref, ref, send.at[1 + h, i], recv.at[1 + h, i], beyond if h else g, across)

        def core_z(i):
            ref = place(block(i, ypos))
            return dma(ref, ref, send.at[3, i], recv.at[3, i], g, sib)

        def core_y(i, h):
            ref = place(block(i, 1 - ypos), h)
            return dma(ref, ref, send.at[4 + h, i], recv.at[4 + h, i], g, sib)

        def start():
            z_copy(1).start()
            z_copy(3).start()
            y_copy(0, 0).start()
            y_copy(0, 1).start()
            core_z(0).start()

        def start_far():
            z_copy(2).start()

        def relay_z(i):
            z_copy(i).wait_recv()
            y_copy(i, 0).start()
            y_copy(i, 1).start()
            core_z(i).start()

        def relay_y(i):
            for h in range(2):
                y_copy(i, h).wait_recv()
                core_y(i, h).start()

        def arrived():
            for i in range(4):
                core_z(i).wait_recv()
                core_y(i, 0).wait_recv()
                core_y(i, 1).wait_recv()

        def finish():
            for i in range(4):
                if i:
                    z_copy(i).wait_send()
                core_z(i).wait_send()
                for h in range(2):
                    y_copy(i, h).wait_send()
                    core_y(i, h).wait_send()

        return start, start_far, relay_z, relay_y, arrived, finish

    mirror = (pair, 2 * g + core)
    barrier = pltpu.get_barrier_semaphore()

    def greet(group, shard):
        pl.semaphore_signal(barrier, inc=1, device_id=(group, shard), device_id_type=MESH)

    for i in range(1, 2 * n):
        greet(g, lax.rem(s + i, 2 * n))
    for i in range(1, n):
        greet(lax.rem(g + i, n), s)

    @pl.when(pair != g)
    def _():
        greet(*mirror)

    greet(beyond, across)

    small = [
        pltpu.make_async_copy(dw_hbm, dw, ios.at[4]),
        pltpu.make_async_copy(up_hbm, up.at[pl.ds(pl.multiple_of(s * 32, 32), 32)], ios.at[5]),
        pltpu.make_async_copy(down_hbm, down.at[pl.ds(pl.multiple_of(s * 128, 128), 128)], ios.at[6]),
        pltpu.make_async_copy(gain_hbm, gain, ios.at[7]),
    ]
    for copy in small[:2]:
        copy.start()
    img_copy.start()
    cot_copy.start()
    for copy in small[2:]:
        copy.start()
    small[0].wait()

    flat[...] = jnp.zeros_like(flat)
    flat[0:49, :] = dw[...].astype(F32).T
    dwb[s] = jnp.concatenate([flat[16 * t : 16 * t + 16, :] for t in range(4)], axis=1).astype(BF16)
    img_copy.wait()
    fill_images(x2, img)
    for copy in small[1:]:
        copy.wait()

    def up_place(j, h=None):
        return up.at[pl.ds(pl.multiple_of(j * 32 + (h or 0) * 16, 16), 32 if h is None else 16)]

    def down_place(j, h=None):
        return down.at[pl.ds(pl.multiple_of(j * 128 + (h or 0) * 64, 64), 128 if h is None else 64)]

    up_start, up_far, up_relay_z, up_relay_y, up_arrived, up_finish = spread(up_place, ups, upr)
    down_start, down_far, down_relay_z, down_relay_y, down_arrived, down_finish = spread(down_place, downs, downr)

    part = chunk // 2

    def ag_place(j, h):
        return ag.at[lax.rem(j, 2), pl.ds(pl.multiple_of(lax.div(j, 2) * chunk + h * part, part), part)]

    gathers = [gather(ag_place(s, h), lambda j, h=h: ag_place(j, h), es, er, 2 * h) for h in range(2)]

    def dw_copy(i):
        return dma(dwb.at[s], dwb.at[s], dws.at[i], dwr.at[i], g, lax.rem(s + i, 2 * n))

    pl.semaphore_wait(barrier, 3 * n - jnp.where(pair == g, 1, 0))
    for i in range(1, 2 * n):
        dw_copy(i).start()
    up_start()
    up_far()
    down_start()
    cot_copy.wait()
    flat_rows(cot, rhs)
    for i in range(1, 2 * n):
        dw_copy(i).wait_recv()
    lane = lax.broadcasted_iota(jnp.int32, (16, 128), 1)
    for blk in range(4):
        lines = [dwb[4 * blk + t].astype(F32) for t in range(4)]
        for k in range(4):
            line = jnp.zeros((16, 128), F32)
            for t in range(4):
                moved = lines[t] if t == k else pltpu.roll(lines[t], 32 * ((t - k) % 4), 1)
                line = jnp.where((lane >= 32 * t) & (lane < 32 * t + 32), moved, line)
            w2[pl.ds(128 * k + blk, 16, stride=8), :] = line
            w2[pl.ds(128 * k + blk + 4, 16, stride=8), :] = line

    def conv_rows(lo, hi):
        @pl.loop(lo, hi)
        def _(h):
            conv_row(x2, w2, c2, h, False)

    conv_rows(0, 4)
    up_relay_z(1)
    up_relay_z(3)
    up_relay_z(2)
    down_far()
    conv_rows(4, 12)
    up_relay_y(0)
    up_relay_y(1)
    up_relay_y(3)
    conv_rows(12, HROWS)
    down_relay_z(1)
    down_relay_z(3)
    norm_rows(c2, xhat, rstd, 0, 4)
    up_relay_y(2)
    norm_rows(c2, xhat, rstd, 4, 7)
    scale_rows(xhat, gain, lhs)
    down_relay_z(2)
    up_arrived()

    def up_steps(lo, hi):
        @pl.loop(lo, hi)
        def _(j):
            up_step(lhs, up, slope, j)

    up_steps(0, 4)
    down_relay_y(0)
    down_relay_y(1)
    down_relay_y(3)
    up_steps(4, 7)
    down_relay_y(2)
    up_steps(7, 8)
    down_arrived()

    @pl.loop(0, 8)
    def _(j):
        back_step(rhs, down, slope, j)

    own = pl.ds(pl.multiple_of(core * half, half), half)
    other = pl.ds(pl.multiple_of((1 - core) * half, half), half)
    scale = (2 * n * PIX) ** -0.5

    def slot(i):
        k, same = lax.rem(i, 4), lax.div(i, 4)
        return 2 * lax.rem(zpos + k + 1, 4) + ypos + (1 - same) * (1 - 2 * ypos)

    def along(k):
        return 4 * lax.rem(zpos + k + 1, 4) + 2 * ypos + core

    first, rest = pl.ds(0, FIRST), pl.ds(FIRST, half - FIRST)

    def a0_copy(i):
        return dma(p.at[i, other], a0.at[i], a0s.at[i], a0r.at[i], g, sib)

    def ya_copy(k):
        return dma(q.at[k, first], ya.at[k], yas.at[k], yar.at[k], g, across)

    def za_copy(k):
        return dma(qa.at[k], za.at[k], zas.at[k], zar.at[k], g, along(k))

    def zb_copy(i):
        return dma(q.at[i, rest], zb.at[i], zbs.at[i], zbr.at[i], g, along(lax.rem(i, 4)))

    yb_copy = dma(qb, yb, ybs, ybr, g, across)

    def pass_on(i):
        a0_copy(i).wait_recv()
        q[i] = (p[i, own].astype(F32) + a0[i].astype(F32)).astype(BF16)

        @pl.when(lax.rem(i, 4) < 3)
        def _():
            zb_copy(i).start()

        @pl.when(i < 4)
        def _():
            ya_copy(i).start()

    def turn_first(k):
        ya_copy(k).wait_recv()
        qa[k] = (q[4 + k, first].astype(F32) + ya[k].astype(F32)).astype(BF16)
        za_copy(k).start()

    def rest_sum(base):
        acc = q[base + 3, rest].astype(F32)
        for k in range(3):
            zb_copy(base + k).wait_recv()
            acc = acc + zb[base + k].astype(F32)
        return acc

    @pl.loop(0, n)
    def _(i):
        p[i] = grad_tile(lhs, rhs, owner[slot(i)], scale).astype(BF16)
        a0_copy(i).start()

        @pl.when(i > 0)
        def _():
            pass_on(i - 1)

    @pl.loop(0, 2)
    def _(j):
        branch_cols(lhs, down, wide, j)

    a0_copy(n - 1).wait_recv()
    q[n - 1] = (p[n - 1, own].astype(F32) + a0[n - 1].astype(F32)).astype(BF16)
    mix_rows(img, wide, mixed)
    mixed_copy.start()
    turn_first(0)

    @pl.loop(0, 2)
    def _(j):
        back_u_cols(rhs, up, wide, j)

    turn_first(1)
    norm_back_rows(wide, xhat, rstd, gain)
    fill_back(x2, wide)
    turn_first(2)
    conv_back_rows(x2, w2, c2, cot, out, 0, 3)
    qb[...] = rest_sum(0).astype(BF16)
    yb_copy.start()
    conv_back_rows(x2, w2, c2, cot, out, 3, 5)

    acc = rest_sum(4)
    yb_copy.wait_recv()
    gfull[pl.ds(pl.multiple_of(core * half + FIRST, 16), half - FIRST)] = (acc + yb[...].astype(F32)).astype(BF16)
    ya_copy(3).wait_recv()
    acc = q[n - 1, first].astype(F32) + ya[3].astype(F32)
    for k in range(3):
        za_copy(k).wait_recv()
        acc = acc + za[k].astype(F32)
    gfull[pl.ds(pl.multiple_of(core * half, 16), FIRST)] = acc.astype(BF16)
    g_copy = dma(gfull.at[own], gfull.at[own], gs, gr, g, sib)
    g_copy.start()
    g_copy.wait_recv()
    whole = gfull[...]
    side = jnp.where(core == 0, whole, whole.T)
    stat = lax.dot_general(side, side, NT, preferred_element_type=F32)
    stat = (stat * (1.0 / tile)).astype(BF16)
    for b, (i, j) in enumerate(PAIRS):
        m[128 * b : 128 * b + 128, :] = stat[128 * i : 128 * i + 128, 128 * j : 128 * j + 128]

    def m_part(j, h):
        return pl.ds(pl.multiple_of(j * chunk + h * part, part), part)

    def c_copy(i, h):
        j = lax.rem(g + i, n)
        return dma(m.at[m_part(j, h)], c1.at[i, pl.ds(h * part, part)], cs.at[h, i], cr.at[h, i], j, s)

    def d_copy(h):
        return dma(c1.at[0, pl.ds(h * part, part)], ag_place(mirror[1], h), ds.at[h], dr.at[h], *mirror)

    for h in range(2):
        for i in range(1, n):
            c_copy(i, h).start()
    conv_back_rows(x2, w2, c2, cot, out, 5, 9)
    for h in range(2):
        acc = m[m_part(g, h), :].astype(F32)
        for i in range(1, n):
            c_copy(i, h).wait_recv()
            acc = acc + c1[i, part * h : part * h + part, :].astype(F32)
        total = acc.astype(BF16)
        c1[0, part * h : part * h + part, :] = total

        @pl.when(pair != g)
        def _():
            d_copy(h).start()

        @pl.when(pair == g)
        def _():
            ag[core, m_part(g, h), :] = total

    conv_back_rows(x2, w2, c2, cot, out, 9, 11)
    for h in range(2):

        @pl.when(pair != g)
        def _():
            d_copy(h).wait_recv()

        gathers[h][0]()

    conv_back_rows(x2, w2, c2, cot, out, 11, HROWS)
    out_copy.start()
    for h in range(2):
        gathers[h][1]()
    for h in range(2):
        gathers[h][2]()

    mixed_copy.wait()
    out_copy.wait()
    up_finish()
    down_finish()
    for h in range(2):
        gathers[h][3]()
    for i in range(1, 2 * n):
        dw_copy(i).wait_send()
    for i in range(n):
        a0_copy(i).wait_send()
    for i in range(n - 1):
        c_copy(i + 1, 0).wait_send()
        c_copy(i + 1, 1).wait_send()
    for i in range(4):
        ya_copy(i).wait_send()
    for i in range(3):
        za_copy(i).wait_send()
        zb_copy(i).wait_send()
        zb_copy(4 + i).wait_send()
    yb_copy.wait_send()
    g_copy.wait_send()

    @pl.when(pair != g)
    def _():
        d_copy(0).wait_send()
        d_copy(1).wait_send()


def local(images, cotangent, dw_kernel, norm_gain, w_up, w_down, owner_table):
    n = lax.axis_size("group")
    half, chunk = BLK // 2, len(PAIRS) * 128 // n
    sem = pltpu.SemaphoreType.DMA
    vmem = pltpu.VMEM
    width = images.shape[-1]
    mixed, back, packed = pl.pallas_call(
        functools.partial(block_kernel, n),
        out_shape=(
            jax.ShapeDtypeStruct((ROWS, COLS, width), BF16),
            jax.ShapeDtypeStruct((ROWS, COLS, width), BF16),
            jax.ShapeDtypeStruct((2, n * chunk, 128), BF16),
        ),
        in_specs=[pl.BlockSpec(memory_space=pl.ANY)] * 6 + [pl.BlockSpec(memory_space=pltpu.SMEM)],
        out_specs=[pl.BlockSpec(memory_space=pl.ANY)] * 2 + [pl.BlockSpec(memory_space=vmem)],
        scratch_shapes=[
            vmem((XROWS * XCOLS * 8, 128), F32),
            vmem((512, 128), F32),
            vmem((HROWS * COLS * 8, 128), F32),
            vmem((PIX, width), F32),
            vmem((PIX, 128), F32),
            vmem((5, PIX, width), BF16),
            vmem((5, PIX, width), BF16),
            vmem((512, 2048), BF16),
            vmem((2048, 512), BF16),
            vmem((8, PIX, 256), F32),
            vmem((PIX, width), F32),
            vmem((2 * n, 16, 128), BF16),
            vmem((64, 32), F32),
            vmem((n, BLK, BLK), BF16),
            vmem((n, half, BLK), BF16),
            vmem((n, half, BLK), BF16),
            vmem((4, FIRST, BLK), BF16),
            vmem((3, FIRST, BLK), BF16),
            vmem((3, FIRST, BLK), BF16),
            vmem((7, half - FIRST, BLK), BF16),
            vmem((half - FIRST, BLK), BF16),
            vmem((half - FIRST, BLK), BF16),
            vmem((BLK, BLK), BF16),
            vmem((n * chunk, 128), BF16),
            vmem((n, chunk, 128), BF16),
            vmem((ROWS, COLS, width), BF16),
            vmem((ROWS, COLS, width), BF16),
            vmem((ROWS, COLS, width), BF16),
            vmem((ROWS, COLS, width), BF16),
            vmem((32, 49), BF16),
            vmem((1, width), F32),
            sem((2 * n,)), sem((2 * n,)),
            sem((6, 4)), sem((6, 4)),
            sem((6, 4)), sem((6, 4)),
            sem((n,)), sem((n,)),
            sem((4,)), sem((4,)),
            sem((3,)), sem((3,)),
            sem((7,)), sem((7,)),
            sem, sem,
            sem, sem,
            sem((2, n)), sem((2, n)),
            sem((2,)), sem((2,)),
            sem((4, n)), sem((4, n)),
            sem((8,)),
        ],
        compiler_params=pltpu.CompilerParams(collective_id=0, has_side_effects=True, vmem_limit_bytes=60 * 2**20),
    )(images[0], cotangent[0], dw_kernel.T, norm_gain.reshape(1, width), w_up, w_down, owner_table)
    mixed, back, stat = pl.pallas_call(
        finish_kernel,
        out_shape=(
            jax.ShapeDtypeStruct((ROWS, COLS, width), BF16),
            jax.ShapeDtypeStruct((ROWS, COLS, width), BF16),
            jax.ShapeDtypeStruct((2, BLK, BLK), F32),
        ),
        in_specs=[pl.BlockSpec(memory_space=pl.ANY)] * 3,
        out_specs=[pl.BlockSpec(memory_space=pl.ANY)] * 3,
        scratch_shapes=[
            vmem((8, 7, COLS, width), BF16),
            vmem((2, n * chunk, 128), BF16),
            vmem((2, BLK, BLK), F32),
            sem((9,)), sem((10,)),
        ],
        compiler_params=pltpu.CompilerParams(vmem_limit_bytes=60 * 2**20),
    )(mixed, back, packed)
    return (mixed[None], back[None], stat[None])


def solution(mesh):
    return jax.shard_map(
        local,
        mesh=mesh,
        in_specs=(
            P(("group", "shard"), None, None, None),
            P(("group", "shard"), None, None, None),
            P(None, "shard"),
            P(),
            P("shard", None),
            P("shard", None),
            P(),
        ),
        out_specs=(
            P(("group", "shard"), None, None, None),
            P(("group", "shard"), None, None, None),
            P("group", None, None, None),
        ),
        check_vma=False,
    )
```
